32 devices in a mesh: dp: 16 (over z, y, core), mp: 2 (over x).
Axes of the slice: x: 2, y: 2, z: 4, core: 2. Of those that a mesh axis runs over, the one named last changes fastest.
Arguments:
- upper_first: bfloat16 [4096, 4096], P('dp'), may hold values from -6 to 6
- upper_second: bfloat16 [4096, 4096], P('dp'), may hold values from -24 to 24
- grad_first: bfloat16 [4096, 4096], P('dp'), may hold values from -6 to 6
- grad_second: bfloat16 [4096, 4096], P('dp'), may hold values from -6 to 6
- norm_gain: bfloat16 [4096], replicated, may hold values from 0.25 to 1.75
- up_weight: bfloat16 [4096, 11264], P('dp', 'mp'), may hold values from -0.09375 to 0.09375
- down_weight: bfloat16 [4096, 11264], P('dp', 'mp'), may hold values from -0.0546875 to 0.0546875
- adapter_down: bfloat16 [4096, 64], replicated, may hold values from -0.09375 to 0.09375
- adapter_up: bfloat16 [64, 4096], replicated, may hold values from -0.75 to 0.75
Outputs:
- lower_first: bfloat16 [4096, 4096], P('dp', 'mp')
- lower_second: bfloat16 [4096, 4096], P('dp', 'mp')
- input_grad_first: bfloat16 [4096, 4096], P('dp', 'mp')
- input_grad_second: bfloat16 [4096, 4096], P('dp')
- adapter_down_grad: float32 [4096, 64], P('mp')
- adapter_up_grad: float32 [64, 4096], P(None, 'mp')
The draws below stay inside these ranges and needn't reach their ends.
All inputs are finite; a program needn't handle non-finite values.
Results may differ from the reference program's by a relative error of at most 0.009.
Values may be sent and summed in bfloat16 or wider, within the bound.
No kernel may reach another device: no remote copies, remote signals or barrier semaphores. Data moves between devices by JAX's collectives and lax.ppermute only.
A program may use at most 192 MiB of HBM per device.

```python
import math
import jax
import jax.numpy as jnp
from jax import lax

D = 4096
FF = 11264
R = 64
TOKENS = 4096
N_MP = 2


def draw_upper_second(key, part):
    first_key, second_key = jax.random.split(jax.random.fold_in(key, 71), 2)
    base = jax.random.normal(first_key, (TOKENS, D), jnp.float32)
    row_scales = jnp.exp(jax.random.uniform(second_key, (TOKENS, 1), jnp.float32, math.log(0.6), math.log(6.0)))
    values = base * row_scales
    return jnp.clip(values, -24.0, 24.0).astype(jnp.bfloat16)


def steps_of(key, shape, pieces, least, high):
    factor_of, own = 1.0, jax.random.fold_in(key, 6)
    for axis_at, parts in pieces:
        heights = jnp.exp(jax.random.uniform(jax.random.fold_in(own, axis_at), (parts,), jnp.float32, least / len(pieces), high / len(pieces)))
        factor_of = factor_of * jnp.repeat(heights, shape[axis_at] // parts).reshape([-1 if axis == axis_at else 1 for axis in range(len(shape))])
    return factor_of


def centred(rng, shape, spread, limit, cuts=(), dtype=jnp.bfloat16):
    drawn = spread * jax.random.normal(rng, shape, jnp.float32)
    if cuts:
        drawn = drawn * steps_of(rng, shape, cuts, -0.22, 0.18)
    return jnp.clip(drawn, -limit, limit).astype(dtype)


def setup_inputs(seed: int = 0) -> dict:
    seeds = jax.random.split(jax.random.key(seed), 10)
    upper_first = centred(seeds[0], (TOKENS, D), 1.0, 6.0, ((0, 16),))
    upper_second = draw_upper_second(jax.random.fold_in(seeds[9], 71), 0)
    grad_first = centred(seeds[2], (TOKENS, D), 1.0, 6.0, ((0, 16),))
    grad_second = centred(seeds[3], (TOKENS, D), 1.0, 6.0, ((0, 16),))
    norm_gain = jnp.clip(1.0 + 0.15 * jax.random.normal(seeds[4], (D,), jnp.float32), 0.25, 1.75).astype(jnp.bfloat16)
    up_weight = centred(seeds[5], (D, FF), D ** -0.5, 0.09375, ((0, 16), (1, 2)))
    down_weight = centred(seeds[6], (D, FF), FF ** -0.5, 0.0546875, ((0, 16), (1, 2)))
    adapter_down = centred(seeds[7], (D, R), D ** -0.5, 0.09375)
    adapter_up = centred(seeds[8], (R, D), R ** -0.5, 0.75)
    return {"upper_first": upper_first, "upper_second": upper_second, "grad_first": grad_first, "grad_second": grad_second, "norm_gain": norm_gain, "up_weight": up_weight, "down_weight": down_weight, "adapter_down": adapter_down, "adapter_up": adapter_up}


def silu_slope(argument):
    sigmoid_value = jax.nn.sigmoid(argument)
    return sigmoid_value * (1.0 + argument * (1.0 - sigmoid_value))

def reference(upper_first, upper_second, grad_first, grad_second, norm_gain, up_weight, down_weight, adapter_down, adapter_up):
    pre_adapter = jnp.dot(upper_first, adapter_down, preferred_element_type=jnp.float32)
    squashed = jax.nn.silu(pre_adapter).astype(jnp.bfloat16)
    adapted = jnp.dot(squashed, adapter_up, preferred_element_type=jnp.float32)
    lower_second = (upper_second.astype(jnp.float32) - adapted).astype(jnp.bfloat16)
    lower_value = lower_second.astype(jnp.float32)
    inverse_rms = lax.rsqrt(lax.optimization_barrier(jnp.mean(lower_value * lower_value, axis=1, keepdims=True)) + 1e-05)
    gain_full = norm_gain.astype(jnp.float32)
    normed = (lower_value * inverse_rms * gain_full).astype(jnp.bfloat16)
    hidden_pre = jnp.dot(normed, up_weight, preferred_element_type=jnp.float32)
    activated = jax.nn.silu(hidden_pre).astype(jnp.bfloat16)
    block_width = FF // N_MP
    frozen_out = jnp.zeros((TOKENS, D), jnp.float32)
    for block in range(N_MP):
        lo_col = block * block_width
        partial_out = jnp.dot(activated[:, lo_col:lo_col + block_width], down_weight[:, lo_col:lo_col + block_width].T, preferred_element_type=jnp.float32)
        rounded = lax.optimization_barrier(partial_out.astype(jnp.bfloat16))
        frozen_out = frozen_out + rounded.astype(jnp.float32)
    lower_first = ((upper_first.astype(jnp.float32) - frozen_out) / 0.5).astype(jnp.bfloat16)
    adapter_slope = jnp.dot(grad_second, adapter_up.T, preferred_element_type=jnp.float32)
    adapter_pre_grad = (adapter_slope * silu_slope(pre_adapter)).astype(jnp.bfloat16)
    carried = (grad_first.astype(jnp.float32) + jnp.dot(adapter_pre_grad, adapter_down.T, preferred_element_type=jnp.float32)).astype(jnp.bfloat16)
    input_grad_first = (0.5 * carried.astype(jnp.float32)).astype(jnp.bfloat16)
    grad_scale = 1.0 / jnp.sqrt(jnp.float32(TOKENS))
    adapter_down_grad = jnp.dot(upper_first.T, adapter_pre_grad, preferred_element_type=jnp.float32) * grad_scale
    adapter_up_grad = jnp.dot(squashed.T, grad_second, preferred_element_type=jnp.float32) * grad_scale
    act_grad = jnp.dot(carried, down_weight, preferred_element_type=jnp.float32)
    pre_grad = (act_grad * silu_slope(hidden_pre)).astype(jnp.bfloat16)
    normed_grad = jnp.dot(pre_grad, up_weight.T, preferred_element_type=jnp.float32)
    curvature = lax.optimization_barrier(jnp.sum(hidden_pre * pre_grad.astype(jnp.float32), axis=1, keepdims=True))
    input_grad_second = (grad_second.astype(jnp.float32) + inverse_rms * gain_full * normed_grad - lower_value * inverse_rms * inverse_rms * curvature / D).astype(jnp.bfloat16)
    return (lower_first, lower_second, input_grad_first, input_grad_second, adapter_down_grad, adapter_up_grad)
```

```python
import math

import jax
import jax.numpy as jnp
from jax import lax
from jax.experimental import pallas as pl
from jax.experimental.pallas import tpu as pltpu
from jax.sharding import PartitionSpec as P

coupling = 0.5


def silu_slope(argument):
    sigmoid_value = jax.nn.sigmoid(argument)
    return sigmoid_value * (1.0 + argument * (1.0 - sigmoid_value))


def after(value, *earlier):
    return lax.optimization_barrier((value, *earlier))[0]


def hop(value, bits):
    size = lax.axis_size("dp")
    return lax.ppermute(value, "dp", [(i, i ^ bits) for i in range(size)])


def swap_mp(value):
    return lax.ppermute(value, "mp", [(0, 1), (1, 0)])


def relative_order(blocks):
    return [(r & ~3) | ((r & 1) << 1) | ((r >> 1) & 1) for r in range(blocks)]


def reorder_body(orders, width, me_ref, *refs):
    count = len(refs) // (1 + len(orders))
    me = me_ref[0]
    for at in range(count):
        source = refs[at]
        for which, (order, flip) in enumerate(orders):
            target = refs[count + at * len(orders) + which]
            for place, block in enumerate(order):
                start = pl.multiple_of((block ^ flip ^ me) * width, width)
                target[:, place * width : (place + 1) * width] = source[:, pl.ds(start, width)]


def reorder(me, arrays, flips, blocks, inverse=False):
    rows, columns = arrays[0].shape
    width = columns // blocks
    order = relative_order(blocks)
    orders = [(order, flip) for flip in flips]
    body = reorder_body
    if inverse:
        body = restore_body
    vmem = pl.BlockSpec(memory_space=pltpu.VMEM)
    return pl.pallas_call(
        lambda *refs: body(orders, width, *refs),
        out_shape=[
            jax.ShapeDtypeStruct(a.shape, a.dtype) for a in arrays for _ in flips
        ],
        in_specs=[pl.BlockSpec(memory_space=pltpu.SMEM)] + [vmem] * len(arrays),
        out_specs=[vmem] * (len(arrays) * len(flips)),
        compiler_params=pltpu.CompilerParams(vmem_limit_bytes=40 * 1024 * 1024),
    )(jnp.reshape(me, (1,)).astype(jnp.int32), *arrays)


def restore_body(orders, width, me_ref, *refs):
    count = len(refs) // 2
    me = me_ref[0]
    for at in range(count):
        for place, block in enumerate(orders[0][0]):
            start = pl.multiple_of((block ^ me) * width, width)
            refs[count + at][:, pl.ds(start, width)] = refs[at][
                :, place * width : (place + 1) * width
            ]


def dot(left, right):
    return jnp.dot(left, right, preferred_element_type=jnp.float32)


def dot_t(left, right):
    return lax.dot_general(
        left, right, (((1,), (1,)), ((), ())), preferred_element_type=jnp.float32
    )


def on_device(
    upper_first,
    upper_second,
    grad_first,
    grad_second,
    norm_gain,
    up_weight,
    down_weight,
    adapter_down,
    adapter_up,
):
    size = lax.axis_size("dp")
    groups = lax.axis_size("mp")
    me = lax.axis_index("dp")
    mp_rank = lax.axis_index("mp")
    tokens, model_width = upper_first.shape
    layers = size // 4
    chunk = model_width // layers
    share_width = model_width // groups
    offset = mp_rank * share_width
    grad_scale = 1.0 / math.sqrt(tokens * size)
    parity = (me >> 2) & 1
    quarter = up_weight.shape[1] // 2

    def halves(weight):
        mine = lax.dynamic_slice_in_dim(weight, parity * quarter, quarter, 1)
        other = lax.dynamic_slice_in_dim(weight, (1 - parity) * quarter, quarter, 1)
        return mine, other

    up_mine, up_other = halves(up_weight)
    down_mine, down_other = halves(down_weight)

    up_z = [up_mine] + [None] * (layers - 1)
    up_y = [None] * layers
    down_z = [down_mine] + [None] * (layers - 1)
    down_y = [None] * layers

    up_z[2] = hop(up_mine, 2 << 2)
    up_z[1] = hop(up_other, 1 << 2)
    up_y[0] = hop(up_mine, 2)
    for s in range(3, layers):
        gate = up_y[0] if s == 3 else up_z[s - 2]
        up_z[s] = hop(after(up_other if s & 1 else up_mine, gate), s << 2)
    for s in range(1, layers):
        up_y[s] = hop(up_z[s], 2)
    down_z[1] = hop(after(down_other, up_z[1], up_y[0]), 1 << 2)
    down_y[0] = hop(after(down_mine, up_y[1]), 2)
    for s in range(2, layers):
        gate = up_z[layers - 2 + (s & 1)] if s < 4 else down_z[s - 2]
        down_z[s] = hop(after(down_other if s & 1 else down_mine, gate), s << 2)
    for s in range(1, layers):
        down_y[s] = hop(down_z[s], 2)

    def whole_chunk(piece, piece_y):
        pair = jnp.concatenate([piece, piece_y], axis=0)
        return jnp.concatenate([pair, hop(pair, 1)], axis=0)

    pre_adapter = dot(upper_first, adapter_down)
    squashed = jax.nn.silu(pre_adapter).astype(jnp.bfloat16)
    adapted = dot(squashed, adapter_up)
    lower_full = (upper_second.astype(jnp.float32) - adapted).astype(jnp.bfloat16)
    lower_value = lower_full.astype(jnp.float32)
    inverse_rms = lax.rsqrt(jnp.mean(lower_value * lower_value, axis=1, keepdims=True) + 1e-05)
    gain_full = norm_gain.astype(jnp.float32)
    normed = (lower_value * inverse_rms * gain_full).astype(jnp.bfloat16)
    adapter_slope = dot_t(grad_second, adapter_up)
    adapter_pre_grad = (adapter_slope * silu_slope(pre_adapter)).astype(jnp.bfloat16)
    back_adapter = dot_t(adapter_pre_grad, adapter_down)
    carried = (grad_first.astype(jnp.float32) + back_adapter).astype(jnp.bfloat16)

    normed_own, normed_send, carried_own, carried_send = reorder(
        me, [normed, carried], [0, 4], size
    )

    def partner_tokens(send):
        part = hop(lax.dynamic_slice_in_dim(send, offset, share_width, 1), 4)
        if groups == 2:
            other = swap_mp(part)
            first = jnp.where(mp_rank == 0, part, other)
            second = jnp.where(mp_rank == 0, other, part)
            return jnp.concatenate([first, second], axis=1)
        return lax.all_gather(part, "mp", axis=1, tiled=True)

    normed_both = jnp.concatenate([normed_own, partner_tokens(normed_send)], axis=0)
    carried_both = jnp.concatenate([carried_own, partner_tokens(carried_send)], axis=0)

    hidden_pre = None
    up_chunks = []
    for s in range(layers):
        up_chunks.append(whole_chunk(up_z[s], up_y[s]))
        term = dot(normed_both[:, s * chunk : (s + 1) * chunk], up_chunks[s])
        hidden_pre = term if s == 0 else hidden_pre + term
    activated = jax.nn.silu(hidden_pre).astype(jnp.bfloat16)

    def summed_pair(parts):
        got = [hop(p[tokens:].astype(jnp.bfloat16), 4) for p in parts]
        return [parts[i][:tokens] + got[i ^ 1].astype(jnp.float32) for i in range(2)]

    act_grad = None
    out_parts = []
    out_sums = []
    for s in range(layers):
        down_chunk = whole_chunk(down_z[s], down_y[s])
        term = dot(carried_both[:, s * chunk : (s + 1) * chunk], down_chunk)
        act_grad = term if s == 0 else act_grad + term
        out_parts.append(dot_t(activated, down_chunk))
        if s & 1:
            out_sums += summed_pair(out_parts[s - 1 : s + 1])
    pre_grad = (act_grad * silu_slope(hidden_pre)).astype(jnp.bfloat16)
    stat_part = jnp.sum(hidden_pre * pre_grad.astype(jnp.float32), axis=1)
    stat_pair = stat_part[:tokens] + hop(stat_part[tokens:], 4)
    curvature = stat_pair + swap_mp(stat_pair) if groups == 2 else lax.psum(stat_pair, "mp")

    grad_sums = []
    for s in range(0, layers, 2):
        pair = summed_pair([dot_t(pre_grad, up_chunks[s]), dot_t(pre_grad, up_chunks[s + 1])])
        for part in pair:
            part = part.astype(jnp.bfloat16)
            if groups == 2:
                total = part.astype(jnp.float32) + swap_mp(part).astype(jnp.float32)
            else:
                total = lax.psum(part.astype(jnp.float32), "mp")
            grad_sums.append(total)

    (out_whole,) = reorder(
        me, [jnp.concatenate(out_sums, axis=1).astype(jnp.bfloat16)], [0], size, inverse=True
    )
    if groups == 2:
        out_keep = lax.dynamic_slice_in_dim(out_whole, offset, share_width, 1)
        out_give = lax.dynamic_slice_in_dim(out_whole, share_width - offset, share_width, 1)
        frozen_share = out_keep.astype(jnp.float32) + swap_mp(out_give).astype(jnp.float32)
    else:
        frozen_share = lax.psum_scatter(
            out_whole.astype(jnp.float32), "mp", scatter_dimension=1, tiled=True
        )
    upper_slice = lax.dynamic_slice_in_dim(upper_first, offset, share_width, 1)
    lower_first = ((upper_slice.astype(jnp.float32) - frozen_share) / coupling).astype(jnp.bfloat16)

    (normed_grad,) = reorder(
        me, [jnp.concatenate(grad_sums, axis=1)], [0], size, inverse=True
    )
    correction = lower_value * inverse_rms * inverse_rms * curvature[:, None] / model_width
    input_grad_second = (
        grad_second.astype(jnp.float32) + inverse_rms * gain_full * normed_grad - correction
    ).astype(jnp.bfloat16)

    lower_second = lax.dynamic_slice_in_dim(lower_full, offset, share_width, 1)
    carried_slice = lax.dynamic_slice_in_dim(carried, offset, share_width, 1)
    input_grad_first = (coupling * carried_slice.astype(jnp.float32)).astype(jnp.bfloat16)

    second_slice = lax.dynamic_slice_in_dim(grad_second, offset, share_width, 1)
    down_grad_part = (
        jnp.einsum("tr,td->rd", adapter_pre_grad, upper_slice, preferred_element_type=jnp.float32)
        * grad_scale
    )
    up_grad_part = (
        jnp.einsum("tr,td->rd", squashed, second_slice, preferred_element_type=jnp.float32)
        * grad_scale
    )
    rank = down_grad_part.shape[0]
    is_core, is_y = (me & 1) == 1, (me & 2) == 2
    keep = jnp.where(is_core, up_grad_part, down_grad_part)
    give = jnp.where(is_core, down_grad_part, up_grad_part)
    keep = keep + hop(give, 1)
    low, high = keep[: rank // 2], keep[rank // 2 :]
    share = jnp.where(is_y, high, low) + hop(jnp.where(is_y, low, high), 2)
    bit = 4
    while bit < size:
        share = share + hop(share, bit)
        bit *= 2
    other = hop(share, 2)
    half = jnp.concatenate(
        [jnp.where(is_y, other, share), jnp.where(is_y, share, other)], axis=0
    )
    other = hop(half, 1)
    adapter_down_grad = jnp.where(is_core, other, half).T
    adapter_up_grad = jnp.where(is_core, half, other)
    return (
        lower_first,
        lower_second,
        input_grad_first,
        input_grad_second,
        adapter_down_grad,
        adapter_up_grad,
    )


def solution(mesh):
    return jax.shard_map(
        on_device,
        mesh=mesh,
        in_specs=(
            P("dp", None),
            P("dp", None),
            P("dp", None),
            P("dp", None),
            P(),
            P("dp", "mp"),
            P("dp", "mp"),
            P(),
            P(),
        ),
        out_specs=(
            P("dp", "mp"),
            P("dp", "mp"),
            P("dp", "mp"),
            P("dp", None),
            P("mp", None),
            P(None, "mp"),
        ),
        check_vma=False,
    )
```

```python
import functools
import math

import jax
import jax.numpy as jnp
from jax import lax
from jax.experimental import pallas as pl
from jax.experimental.pallas import tpu as pltpu
from jax.sharding import PartitionSpec as P

coupling = 0.5
SMEM = pl.BlockSpec(memory_space=pltpu.SMEM)
FREE = pl.CostEstimate(flops=0, bytes_accessed=0, transcendentals=0)
PARAMS = pltpu.CompilerParams(vmem_limit_bytes=56 * 1024 * 1024)


def silu_slope(argument):
    sigmoid_value = jax.nn.sigmoid(argument)
    return sigmoid_value * (1.0 + argument * (1.0 - sigmoid_value))


def after(value, *earlier):
    return lax.optimization_barrier((value, *earlier))[0]


def together(*values):
    return lax.optimization_barrier(values)


def hop(value, bits):
    size = lax.axis_size("dp")
    return lax.ppermute(value, "dp", [(i, i ^ bits) for i in range(size)])


def swap_mp(value):
    return lax.ppermute(value, "mp", [(0, 1), (1, 0)])


def place_of(block, me):
    relative = block ^ (me & ~1)
    return (relative & ~3) | ((relative & 1) << 1) | ((relative >> 1) & 1)


def block_at(place, me):
    return ((place & ~3) | ((place & 1) << 1) | ((place >> 1) & 1)) ^ (me & ~1)


def dot(left, right):
    return jnp.dot(left, right, preferred_element_type=jnp.float32)


def dot_t(left, right):
    return lax.dot_general(
        left, right, (((1,), (1,)), ((), ())), preferred_element_type=jnp.float32
    )


def call(body, cost=FREE, **settings):
    return pl.pallas_call(body, compiler_params=PARAMS, cost_estimate=cost, **settings)


def head_body(blocks, groups, at, uf, us, gf, gs, gain, down_t, up, *outs):
    (squashed_o, apg_o, inverse_o, lower_o, lower_share, input_share) = outs[:6]
    normed_own, normed_send, carried_own, carried_send = outs[6:]
    me, rank = at[0], at[1]
    width = uf.shape[1]
    column = width // blocks
    share = width // groups
    pre = dot_t(uf[...], down_t[...])
    squashed = (pre * jax.nn.sigmoid(pre)).astype(jnp.bfloat16)
    squashed_o[...] = squashed
    lower = (us[...].astype(jnp.float32) - dot(squashed, up[...])).astype(jnp.bfloat16)
    lower_o[...] = lower
    value = lower.astype(jnp.float32)
    inverse = lax.rsqrt(jnp.mean(value * value, axis=1, keepdims=True) + 1e-05)
    inverse_o[...] = jnp.broadcast_to(inverse, inverse_o.shape)
    normed = (value * inverse * gain[...].astype(jnp.float32)).astype(jnp.bfloat16)
    apg = (dot_t(gs[...], up[...]) * silu_slope(pre)).astype(jnp.bfloat16)
    apg_o[...] = apg
    carried = (gf[...].astype(jnp.float32) + dot(apg, down_t[...])).astype(jnp.bfloat16)
    for group in range(groups):

        @pl.when(rank == group)
        def _():
            part = slice(group * share, (group + 1) * share)
            lower_share[...] = lower[:, part]
            input_share[...] = (coupling * carried[:, part].astype(jnp.float32)).astype(
                jnp.bfloat16
            )

    for block in range(blocks):
        part = slice(block * column, (block + 1) * column)
        own = pl.multiple_of(place_of(block, me) * column, column)
        normed_own[:, pl.ds(own, column)] = normed[:, part]
        carried_own[:, pl.ds(own, column)] = carried[:, part]
        place = place_of(block, me ^ 4) * column - rank * share

        @pl.when((place >= 0) & (place < share))
        def _():
            to = pl.multiple_of(place, column)
            normed_send[:, pl.ds(to, column)] = normed[:, part]
            carried_send[:, pl.ds(to, column)] = carried[:, part]


def head(at, blocks, groups, uf, us, gf, gs, gain, down_t, up):
    tokens, width = uf.shape
    rank = up.shape[0]
    share = width // groups
    step = 64 if tokens % 64 == 0 else tokens
    row = lambda columns: pl.BlockSpec((step, columns), lambda i: (i, 0))
    whole = lambda a: pl.BlockSpec(a.shape, lambda i: (0, 0))
    outs = [rank, rank, 128, width, share, share, width, share, width, share]
    types = [jnp.bfloat16, jnp.bfloat16, jnp.float32] + [jnp.bfloat16] * 7
    return call(
        functools.partial(head_body, blocks, groups),
        grid=(tokens // step,),
        in_specs=[SMEM] + [row(width)] * 4 + [whole(gain), whole(down_t), whole(up)],
        out_specs=[row(c) for c in outs],
        out_shape=[jax.ShapeDtypeStruct((tokens, c), t) for c, t in zip(outs, types)],
    )(at, uf, us, gf, gs, gain, down_t, up)


def both_body(at, own, part, other, out):
    tokens, share = part.shape
    out[:tokens] = own[...]
    for group in range(2):
        place = group * share

        @pl.when(at[1] == group)
        def _():
            out[tokens:, place : place + share] = part[...]
            out[tokens:, share - place : 2 * share - place] = other[...]


def both_tokens(at, own, part, other):
    tokens, width = own.shape
    return call(
        both_body,
        in_specs=[SMEM] + [pl.BlockSpec(memory_space=pltpu.VMEM)] * 3,
        out_specs=pl.BlockSpec(memory_space=pltpu.VMEM),
        out_shape=jax.ShapeDtypeStruct((2 * tokens, width), own.dtype),
    )(at, own, part, other)


def stack(*units):
    columns, dtype = units[0][0].shape[1], units[0][0].dtype
    arrays = []
    for array, _, _ in units:
        if not any(array is a for a in arrays):
            arrays.append(array)
    which = [next(k for k, a in enumerate(arrays) if a is u[0]) for u in units]
    total = sum(u[2] for u in units)

    def body(*refs):
        out, held, got, put = refs[-4:]
        reads, writes, at = [], [], 0
        for i, (_, first, rows) in enumerate(units):
            here = held.at[pl.ds(at, rows)]
            reads.append(
                pltpu.make_async_copy(refs[which[i]].at[pl.ds(first, rows)], here, got.at[i])
            )
            writes.append(pltpu.make_async_copy(here, out.at[pl.ds(at, rows)], put.at[i]))
            at += rows
        for read in reads:
            read.start()
        for read, write in zip(reads, writes):
            read.wait()
            write.start()
        for write in writes:
            write.wait()

    anywhere = pl.BlockSpec(memory_space=pl.ANY)
    return call(
        body,
        in_specs=[anywhere] * len(arrays),
        out_specs=anywhere,
        out_shape=jax.ShapeDtypeStruct((total, columns), dtype),
        scratch_shapes=[
            pltpu.VMEM((total, columns), dtype),
            pltpu.SemaphoreType.DMA((len(units),)),
            pltpu.SemaphoreType.DMA((len(units),)),
        ],
    )(*arrays)


ANY = pl.BlockSpec(memory_space=pl.ANY)


def fetch(units, refs, held, sems):
    copies, at = [], 0
    for i, (_, first, rows) in enumerate(units):
        copies.append(
            pltpu.make_async_copy(
                refs[i].at[pl.ds(first, rows)], held.at[pl.ds(at, rows)], sems.at[i]
            )
        )
        at += rows
    for copy in copies:
        copy.start()
    for copy in copies:
        copy.wait()


def held_scratch(units):
    array = units[0][0]
    return [
        pltpu.VMEM((sum(u[2] for u in units), array.shape[1]), array.dtype),
        pltpu.SemaphoreType.DMA((len(units),)),
    ]


def both_halves(tokens, step, columns, use):
    for which in range(2):

        @pl.when(step == which)
        def _():
            use(tokens[which][:, columns])


def hidden_body(units, *refs):
    count = len(units)
    tokens, refs = refs[:2], refs[2:]
    hidden, slope, activated, held, sems = refs[count:]
    step = pl.program_id(0)

    @pl.when(step == 0)
    def _():
        fetch(units, refs, held, sems)

    def use(left):
        total = dot(left, held[...])
        hidden[...] = total
        sigmoid_value = jax.nn.sigmoid(total)
        slope[...] = sigmoid_value * (1.0 + total * (1.0 - sigmoid_value))
        activated[...] = (total * sigmoid_value).astype(jnp.bfloat16)

    both_halves(tokens, step, slice(None), use)


def hidden_kernel(tokens, units):
    count, width = tokens[0].shape
    columns = units[0][0].shape[1]
    whole = pl.BlockSpec((count, width), lambda i: (0, 0))
    out = pl.BlockSpec((count, columns), lambda i: (i, 0))
    return call(
        functools.partial(hidden_body, units),
        cost=work(4 * count * columns * width),
        grid=(2,),
        in_specs=[whole, whole] + [ANY] * len(units),
        out_specs=[out] * 3,
        out_shape=[
            jax.ShapeDtypeStruct((2 * count, columns), t)
            for t in (jnp.float32, jnp.float32, jnp.bfloat16)
        ],
        scratch_shapes=held_scratch(units),
    )(*tokens, *[u[0] for u in units])


def act_body(units, spans, extras, slope_given, *refs):
    count = len(units)
    tokens, refs = refs[:2], refs[2:]
    outs, (held, sems) = refs[count + extras : -2], refs[-2:]
    step = pl.program_id(0)

    @pl.when(step == 0)
    def _():
        fetch(units, refs, held, sems)

    for which in range(2):
        out = outs[which % len(outs)]

        @pl.when(step == which)
        def _():
            total, at = None, 0
            for first, depth in spans:
                term = dot(tokens[which][:, first : first + depth], held[at : at + depth])
                total = term if total is None else total + term
                at += depth
            if extras > slope_given:
                total = total + refs[count][...]
            if slope_given:
                total = total * refs[count + extras - 1][...]
            out[...] = total.astype(out.dtype)


def work(flops):
    return pl.CostEstimate(flops=flops // 4, bytes_accessed=0, transcendentals=0)


def act_kernel(tokens, spans, partial, slope=None):
    count, width = tokens[0].shape
    merged = []
    for first, us in spans:
        depth = sum(u[2] for u in us)
        if merged and sum(merged[-1]) == first:
            merged[-1] = (merged[-1][0], merged[-1][1] + depth)
        else:
            merged.append((first, depth))
    units = [u for _, us in spans for u in us]
    columns = units[0][0].shape[1]
    whole = pl.BlockSpec((count, width), lambda i: (0, 0))
    out = pl.BlockSpec((count, columns), lambda i: (i, 0))
    extra = [a for a in (partial, slope) if a is not None]
    half = pl.BlockSpec((count, columns), lambda i: (0, 0))
    if slope is None:
        out_specs, out_shape = out, jax.ShapeDtypeStruct((2 * count, columns), jnp.float32)
    else:
        out_specs = [half, half]
        out_shape = [jax.ShapeDtypeStruct((count, columns), jnp.bfloat16)] * 2
    return call(
        functools.partial(act_body, units, merged, len(extra), int(slope is not None)),
        cost=work(4 * count * columns * sum(d for _, d in merged)),
        grid=(2,),
        in_specs=[whole, whole] + [ANY] * len(units) + [out] * len(extra),
        out_specs=out_specs,
        out_shape=out_shape,
        scratch_shapes=held_scratch(units),
    )(*tokens, *[u[0] for u in units], *extra)


def stat_body(hidden, pre_grad, out):
    out[...] = jnp.sum(hidden[...] * pre_grad[...].astype(jnp.float32), axis=1, keepdims=True)


def stat_kernel(hidden, pre_grad):
    count, columns = hidden.shape
    step = count // 4
    block = pl.BlockSpec((step, columns), lambda i: (i, 0))
    return call(
        stat_body,
        grid=(4,),
        in_specs=[block, block],
        out_specs=pl.BlockSpec((step, 1), lambda i: (i, 0)),
        out_shape=jax.ShapeDtypeStruct((count, 1), jnp.float32),
    )(hidden, pre_grad)


def out_body(units, left, *refs):
    own, other, held, sems = refs[len(units) :]
    step = pl.program_id(0)

    @pl.when(step == 0)
    def _():
        fetch(units, refs, held, sems)
        own[...] = dot_t(left[...], held[...])

    @pl.when(step == 1)
    def _():
        other[...] = dot_t(left[...], held[...]).astype(jnp.bfloat16)


def out_kernel(left, units):
    count, depth = left.shape
    columns = sum(u[2] for u in units)
    out = pl.BlockSpec((count // 2, columns), lambda i: (0, 0))
    return call(
        functools.partial(out_body, units),
        cost=work(2 * count * columns * depth),
        grid=(2,),
        in_specs=[pl.BlockSpec((count // 2, depth), lambda i: (i, 0))] + [ANY] * len(units),
        out_specs=[out, out],
        out_shape=[
            jax.ShapeDtypeStruct((count // 2, columns), jnp.float32),
            jax.ShapeDtypeStruct((count // 2, columns), jnp.bfloat16),
        ],
        scratch_shapes=held_scratch(units),
    )(left, *[u[0] for u in units])


def final_body(blocks, layers, at, gs, lower, gain, inverse, curvature, *refs):
    mine, got, out = refs[:layers], refs[layers:-1], refs[-1]
    me = at[0]
    width = out.shape[1]
    column = width // blocks
    scale = inverse[...][:, :1]
    drop = scale * scale * curvature[...] / width
    for place in range(blocks):
        layer, inner = divmod(place * column, mine[0].shape[1])
        part = slice(inner, inner + column)
        grad = mine[layer][:, part].astype(jnp.float32) + got[layer][:, part].astype(jnp.float32)
        spot = pl.ds(pl.multiple_of(block_at(place, me) * column, column), column)
        out[:, spot] = (
            gs[:, spot].astype(jnp.float32)
            + scale * gain[:, spot].astype(jnp.float32) * grad
            - lower[:, spot].astype(jnp.float32) * drop
        ).astype(jnp.bfloat16)


def final_kernel(at, blocks, gs, lower, gain, inverse, curvature, mine, got):
    tokens, width = gs.shape
    step = 64 if tokens % 64 == 0 else tokens
    row = lambda a: pl.BlockSpec((step, a.shape[1]), lambda i: (i, 0))
    return call(
        functools.partial(final_body, blocks, len(mine)),
        grid=(tokens // step,),
        in_specs=[SMEM, row(gs), row(lower), pl.BlockSpec(gain.shape, lambda i: (0, 0))]
        + [row(a) for a in [inverse, curvature, *mine, *got]],
        out_specs=row(gs),
        out_shape=jax.ShapeDtypeStruct(gs.shape, jnp.bfloat16),
    )(at, gs, lower, gain, inverse, curvature, *mine, *got)


def restore_body(blocks, layers, at, *refs):
    out = refs[layers]
    column = out.shape[1] // blocks
    for place in range(blocks):
        layer, inner = divmod(place * column, refs[0].shape[1])
        spot = pl.multiple_of(block_at(place, at[0]) * column, column)
        out[:, pl.ds(spot, column)] = refs[layer][:, inner : inner + column]


def restore(at, blocks, arrays):
    vmem = pl.BlockSpec(memory_space=pltpu.VMEM)
    tokens, chunk = arrays[0].shape
    return call(
        functools.partial(restore_body, blocks, len(arrays)),
        in_specs=[SMEM] + [vmem] * len(arrays),
        out_specs=vmem,
        out_shape=jax.ShapeDtypeStruct((tokens, chunk * len(arrays)), arrays[0].dtype),
    )(at, *arrays)


def first_body(blocks, at, upper, *refs):
    sums, got, out = refs[:4], refs[4:8], refs[8]
    me, rank = at[0], at[1]
    share = out.shape[1]
    chunk = share // 2
    column = 2 * share // blocks
    pair = (rank ^ (me >> 3)) & 1
    for which in range(2):

        @pl.when(pair == which)
        def _():
            for place in range(which * blocks // 2, (which + 1) * blocks // 2):
                layer, part = divmod(place * column, chunk)
                block = block_at(place, me)
                spot = pl.multiple_of(block * column, column)
                to = pl.multiple_of(block * column - rank * share, column)
                columns = slice(part, part + column)
                frozen = sums[layer][:, columns].astype(jnp.float32) + got[layer][
                    :, columns
                ].astype(jnp.float32)
                out[:, pl.ds(to, column)] = (
                    (upper[:, pl.ds(spot, column)].astype(jnp.float32) - frozen) / coupling
                ).astype(jnp.bfloat16)


def first_kernel(at, blocks, upper, sums, got):
    tokens, width = upper.shape
    step = 64 if tokens % 64 == 0 else tokens
    row = lambda columns: pl.BlockSpec((step, columns), lambda i: (i, 0))
    return call(
        functools.partial(first_body, blocks),
        grid=(tokens // step,),
        in_specs=[SMEM, row(width)] + [row(a.shape[1]) for a in [*sums, *got]],
        out_specs=row(width // 2),
        out_shape=jax.ShapeDtypeStruct((tokens, width // 2), jnp.bfloat16),
    )(at, upper, *sums, *got)


def on_device(
    upper_first,
    upper_second,
    grad_first,
    grad_second,
    norm_gain,
    up_weight,
    down_weight,
    adapter_down,
    adapter_up,
):
    size = lax.axis_size("dp")
    groups = lax.axis_size("mp")
    me = lax.axis_index("dp")
    mp_rank = lax.axis_index("mp")
    at = jnp.stack([me, mp_rank]).astype(jnp.int32)
    tokens, model_width = upper_first.shape
    layers = size // 4
    share_width = model_width // groups
    offset = mp_rank * share_width
    grad_scale = 1.0 / math.sqrt(tokens * size)
    parity = (me >> 2) & 1
    quarter = up_weight.shape[1] // 2
    gain = norm_gain.reshape(1, model_width)
    paired = groups == 2 and layers == 4

    rows = up_weight.shape[0]
    chunk = 4 * rows
    far = range(3, layers)
    eighth = quarter // 2
    core = me & 1

    def cut(weight):
        mine = lax.dynamic_slice_in_dim(weight, core * quarter, quarter, 1)
        other = lax.dynamic_slice_in_dim(weight, (1 - core) * quarter, quarter, 1)
        return mine, other

    def by_parity(own, got):
        first = jnp.where(core == 0, own, got)
        pair = jnp.concatenate([first, jnp.where(core == 0, got, own)], axis=0)
        mine = lax.dynamic_slice_in_dim(pair, parity * eighth, eighth, 1)
        other = lax.dynamic_slice_in_dim(pair, (1 - parity) * eighth, eighth, 1)
        return mine, other

    def of_z(pair, s):
        return pair[s & 1]

    def units_of(piece, piece_y, first=0, count=2):
        return [(a, u * rows, rows) for u in range(first, first + count) for a in (piece, piece_y)]

    up_own, up_send = cut(up_weight)
    down_own, down_send = cut(down_weight)
    up_got = hop(up_send, 1)
    down_got = hop(down_send, 1)
    up = by_parity(up_own, up_got)
    (up, (down_own, down_got, upper_first, upper_second, grad_first, grad_second, adapter_up)) = (
        together(
            up,
            (down_own, down_got, upper_first, upper_second, grad_first, grad_second, adapter_up),
        )
    )

    uz, uy, dz, dy = [[None] * layers for _ in range(4)]
    uz[0] = up[0]
    uz[2] = hop(up[0], 2 << 2)
    uz[1] = hop(up[1], 1 << 2)
    uy[0] = hop(up[0], 2)
    down = by_parity(down_own, down_got)
    dz[0] = down[0]
    dy[0] = hop(down[0], 2)
    (
        squashed,
        adapter_pre_grad,
        inverse_rms,
        lower_full,
        lower_second,
        input_grad_first,
        normed_own,
        normed_send,
        carried_own,
        carried_send,
    ) = head(
        at,
        size,
        groups,
        upper_first,
        upper_second,
        grad_first,
        grad_second,
        gain,
        adapter_down.T,
        adapter_up,
    )
    up, down, uz, uy, dz, dy, normed_send, carried_send, adapter_pre_grad, squashed = together(
        up, down, uz, uy, dz, dy, normed_send, carried_send, adapter_pre_grad, squashed
    )

    for s in far:
        uz[s] = hop(of_z(up, s), s << 2)
    normed_part = hop(normed_send, 4)
    uy[2] = hop(uz[2], 2)
    uy[1] = hop(uz[1], 2)
    upper_slice = lax.dynamic_slice_in_dim(upper_first, offset, share_width, 1)
    second_slice = lax.dynamic_slice_in_dim(grad_second, offset, share_width, 1)
    down_grad_part = (
        jnp.einsum("tr,td->rd", adapter_pre_grad, upper_slice, preferred_element_type=jnp.float32)
        * grad_scale
    )
    up_grad_part = (
        jnp.einsum("tr,td->rd", squashed, second_slice, preferred_element_type=jnp.float32)
        * grad_scale
    )
    rank = down_grad_part.shape[0]
    is_core, is_y = (me & 1) == 1, (me & 2) == 2
    keep = jnp.where(is_core, up_grad_part, down_grad_part)
    give = jnp.where(is_core, down_grad_part, up_grad_part)
    uz, uy, normed_part, down, carried_send, keep, give = together(
        uz, uy, normed_part, down, carried_send, keep, give
    )

    low_rows, high_rows = slice(0, rows), slice(rows, 2 * rows)
    dzp = [[None, None] for _ in range(layers)]
    dyp = [[None, None] for _ in range(layers)]
    dzp[2][0] = hop(down[0][low_rows], 2 << 2)
    carried_part = hop(carried_send, 4)
    for s in far:
        uy[s] = hop(uz[s], 2)
    normed_other = swap_mp(normed_part) if groups == 2 else normed_part
    keep = keep + hop(give, 1)
    low, high = keep[: rank // 2], keep[rank // 2 :]
    share, give = jnp.where(is_y, high, low), jnp.where(is_y, low, high)
    dzp, uz, uy, carried_part, normed_part, normed_other, down, normed_own, carried_own, share, give = (
        together(
            dzp, uz, uy, carried_part, normed_part, normed_other, down, normed_own, carried_own,
            share, give,
        )
    )

    dzp[2][1] = hop(down[0][high_rows], 2 << 2)
    dzp[1][0] = hop(down[1][low_rows], 1 << 2)
    dyp[2][0] = hop(dzp[2][0], 2)
    carried_other = swap_mp(carried_part) if groups == 2 else carried_part

    def pair_tokens(own, piece, other):
        if groups == 2:
            return both_tokens(at, own, piece, other)
        return jnp.concatenate([own, lax.all_gather(piece, "mp", axis=1, tiled=True)], axis=0)

    up_units = sum([units_of(uz[s], uy[s]) for s in range(layers)], [])
    normed_both = pair_tokens(normed_own, normed_part, normed_other)
    hidden_pre, slope, activated = hidden_kernel([normed_both, hop(normed_both, 1)], up_units)
    dzp, dyp, carried_part, carried_other, hidden_pre, slope, activated, down, uz, uy, dz, dy = (
        together(
            dzp, dyp, carried_part, carried_other, hidden_pre, slope, activated, down, uz, uy, dz,
            dy,
        )
    )

    for s in far:
        dzp[s][0] = hop(of_z(down, s)[low_rows], s << 2)
    dyp[1][0] = hop(dzp[1][0], 2)
    dzp[1][1] = hop(down[1][high_rows], 1 << 2)
    dyp[2][1] = hop(dzp[2][1], 2)
    carried_both = pair_tokens(carried_own, carried_part, carried_other)
    carried_both = [carried_both, hop(carried_both, 1)]
    out_parts = [None] * layers
    zero = units_of(dz[0], dy[0])
    out_parts[0] = out_kernel(activated, zero)
    partial = act_kernel(carried_both, [(0, zero)], None)
    dzp, dyp, carried_both, out_parts, partial, uz, uy = together(
        dzp, dyp, carried_both, out_parts, partial, uz, uy
    )

    def unit(s, u):
        return [(dzp[s][u], 0, rows), (dyp[s][u], 0, rows)]

    def core_sum(parts):
        own, other = parts
        total = own + hop(other, 1).astype(jnp.float32)
        return total[:tokens], total[tokens:].astype(jnp.bfloat16)

    for s in far:
        dzp[s][1] = hop(of_z(down, s)[high_rows], s << 2)
        dyp[s][0] = hop(dzp[s][0], 2)
    dyp[1][1] = hop(dzp[1][1], 2)
    core_parts, got = [None] * layers, [None] * layers
    core_parts[0] = core_sum(out_parts[0])
    got[1] = hop(core_parts[0][1], 4)
    two = unit(2, 0) + unit(2, 1)
    out_parts[2] = out_kernel(activated, two)
    partial = act_kernel(
        carried_both, [(chunk, unit(1, 0)), (2 * chunk, two)], partial
    )
    up_chunks = [stack(*units_of(uz[s], uy[s])) for s in range(layers)]
    dzp, dyp, core_parts, got, out_parts, partial, up_chunks, hidden_pre, slope, share, give = (
        together(
            dzp, dyp, core_parts, got, out_parts, partial, up_chunks, hidden_pre, slope, share,
            give,
        )
    )

    for s in far:
        dyp[s][1] = hop(dzp[s][1], 2)
    core_parts[2] = core_sum(out_parts[2])
    got[3] = hop(core_parts[2][1], 4)
    one = unit(1, 0) + unit(1, 1)
    out_parts[1] = out_kernel(activated, one)
    partial = act_kernel(
        carried_both,
        [(chunk + chunk // 2, unit(1, 1))] + [(s * chunk, unit(s, 0)) for s in far],
        partial,
    )
    dyp, got, core_parts, out_parts, partial, share, give = together(
        dyp, got, core_parts, out_parts, partial, share, give
    )

    pre_own, pre_other = act_kernel(
        carried_both, [(s * chunk + chunk // 2, unit(s, 1)) for s in far], partial, slope
    )
    core_parts[1] = core_sum(out_parts[1])
    got[0] = hop(core_parts[1][1], 4)
    share = share + hop(give, 2)
    pre_own, pre_other, core_parts, got, hidden_pre, share = together(
        pre_own, pre_other, core_parts, got, hidden_pre, share
    )

    def out_sum(s):
        return (core_parts[s][0] + got[s].astype(jnp.float32)).astype(jnp.bfloat16)

    def to_holder(s):
        moves = []
        for i in range(size):
            holder = ((i >> 3) ^ (s >> 1)) & 1
            moves.append((2 * i + 1 - holder, 2 * i + holder))
        return lax.ppermute(out_sums[s], ("dp", "mp"), moves)

    def product(s):
        other = dot_t(pre_other, up_chunks[s]).astype(jnp.bfloat16)
        return core_sum((dot_t(pre_own, up_chunks[s]), other))

    def share_mp(piece):
        if groups == 2:
            return swap_mp(piece)
        whole = lax.psum(piece.astype(jnp.float32), "mp")
        return whole - piece.astype(jnp.float32)

    out_sums = [None] * layers
    other = half = None
    out_sums[0], out_sums[1] = out_sum(0), out_sum(1)
    sent = [None] * layers
    grads = [None] * layers
    grad_in = [None] * layers
    grad_mine = [None] * layers
    grad_got = [None] * layers
    grads[0] = product(0)
    if paired:
        sent[0] = to_holder(0)
    (grads, out_sums, sent, pre_own, pre_other, share) = together(
        grads, out_sums, sent, pre_own, pre_other, share
    )
    for step in range(layers + 1):
        if step < layers:
            grad_in[step ^ 1] = hop(grads[step][1], 4)
        if step:
            s = (step - 1) ^ 1
            grad_mine[s] = (grads[s][0] + grad_in[s].astype(jnp.float32)).astype(jnp.bfloat16)
            grad_got[s] = share_mp(grad_mine[s])
        if step + 1 < layers:
            grads[step + 1] = product(step + 1)
        if step == 0:
            if paired:
                sent[1] = to_holder(1)
            stat = jnp.concatenate(
                [
                    jnp.sum(hidden_pre[: 2 * tokens] * pre_own.astype(jnp.float32), axis=1),
                    jnp.sum(hidden_pre[2 * tokens :] * pre_other.astype(jnp.float32), axis=1),
                ]
            )[:, None]
            share = share + hop(share, 4)
        if step == 1:
            stat = stat[: 2 * tokens] + hop(stat[2 * tokens :], 1)
            bit = 8
            while bit < size:
                share = share + hop(share, bit)
                bit *= 2
        if step == 2:
            stat = stat[:tokens] + hop(stat[tokens:], 4)
            other = hop(share, 2)
            half = jnp.concatenate(
                [jnp.where(is_y, other, share), jnp.where(is_y, share, other)], axis=0
            )
        if step == 3:
            stat = stat + swap_mp(stat) if groups == 2 else lax.psum(stat, "mp")
            other = hop(half, 1)
        if step == max(layers - 2, 0):
            for s in far:
                out_parts[s] = out_kernel(activated, unit(s, 0) + unit(s, 1))
                core_parts[s] = core_sum(out_parts[s])
        if step == layers - 1:
            out_sums[3] = out_sum(3)
            if paired:
                sent[3] = to_holder(3)
        if step == layers:
            for s in far:
                got[s ^ 1] = hop(core_parts[s][1], 4)
        state = (
            grads, grad_in, grad_mine, grad_got, out_sums, sent, core_parts, got, stat, share,
            other, pre_own, pre_other, hidden_pre,
        )
        (
            grads, grad_in, grad_mine, grad_got, out_sums, sent, core_parts, got, stat, share,
            other, pre_own, pre_other, hidden_pre,
        ) = together(*state)
    curvature = stat
    out_sums = [out_sum(s) if out_sums[s] is None else out_sums[s] for s in range(layers)]
    adapter_down_grad = jnp.where(is_core, other, half).T
    adapter_up_grad = jnp.where(is_core, half, other)

    input_grad_second = final_kernel(
        at,
        size,
        grad_second,
        lower_full,
        gain,
        inverse_rms,
        curvature,
        grad_mine,
        grad_got,
    )

    if paired:
        sent[2] = to_holder(2)
        lower_first = first_kernel(at, size, upper_first, out_sums, sent)
    else:
        out_whole = restore(at, size, out_sums)
        frozen_share = lax.psum_scatter(
            out_whole.astype(jnp.float32), "mp", scatter_dimension=1, tiled=True
        )
        lower_first = ((upper_slice.astype(jnp.float32) - frozen_share) / coupling).astype(
            jnp.bfloat16
        )
    return (
        lower_first,
        lower_second,
        input_grad_first,
        input_grad_second,
        adapter_down_grad,
        adapter_up_grad,
    )


def solution(mesh):
    return jax.shard_map(
        on_device,
        mesh=mesh,
        in_specs=(
            P("dp", None),
            P("dp", None),
            P("dp", None),
            P("dp", None),
            P(),
            P("dp", "mp"),
            P("dp", "mp"),
            P(),
            P(),
        ),
        out_specs=(
            P("dp", "mp"),
            P("dp", "mp"),
            P("dp", "mp"),
            P("dp", None),
            P("mp", None),
            P(None, "mp"),
        ),
        check_vma=False,
    )
```

```python
import functools
import math

import jax
import jax.numpy as jnp
from jax import lax
from jax.experimental import pallas as pl
from jax.experimental.pallas import tpu as pltpu
from jax.sharding import PartitionSpec as P

coupling = 0.5
SMEM = pl.BlockSpec(memory_space=pltpu.SMEM)
FREE = pl.CostEstimate(flops=0, bytes_accessed=0, transcendentals=0)
MIB = 1024 * 1024


def silu_slope(argument):
    sigmoid_value = jax.nn.sigmoid(argument)
    return sigmoid_value * (1.0 + argument * (1.0 - sigmoid_value))


def after(value, *earlier):
    return lax.optimization_barrier((value, *earlier))[0]


def together(*values):
    return lax.optimization_barrier(values)


def hop(value, bits):
    size = lax.axis_size("dp")
    return lax.ppermute(value, "dp", [(i, i ^ bits) for i in range(size)])


def swap_mp(value):
    return lax.ppermute(value, "mp", [(0, 1), (1, 0)])


def place_of(block, me):
    relative = block ^ (me & ~1)
    return (relative & ~3) | ((relative & 1) << 1) | ((relative >> 1) & 1)


def block_at(place, me):
    return ((place & ~3) | ((place & 1) << 1) | ((place >> 1) & 1)) ^ (me & ~1)


def dot(left, right):
    return jnp.dot(left, right, preferred_element_type=jnp.float32)


def dot_t(left, right):
    return lax.dot_general(
        left, right, (((1,), (1,)), ((), ())), preferred_element_type=jnp.float32
    )


def call(body, cost=FREE, room=24, **settings):
    params = pltpu.CompilerParams(vmem_limit_bytes=room * MIB)
    return pl.pallas_call(body, compiler_params=params, cost_estimate=cost, **settings)


def head_body(blocks, groups, at, uf, us, gf, gs, gain, down_t, up, *outs):
    (squashed_o, apg_o, inverse_o, lower_o, lower_share, input_share) = outs[:6]
    normed_own, carried_own, first_send, second_send = outs[6:]
    me, rank = at[0], at[1]
    width = uf.shape[1]
    column = width // blocks
    share = width // groups
    pre = dot_t(uf[...], down_t[...])
    squashed = (pre * jax.nn.sigmoid(pre)).astype(jnp.bfloat16)
    squashed_o[...] = squashed
    lower = (us[...].astype(jnp.float32) - dot(squashed, up[...])).astype(jnp.bfloat16)
    lower_o[...] = lower
    value = lower.astype(jnp.float32)
    inverse = lax.rsqrt(jnp.mean(value * value, axis=1, keepdims=True) + 1e-05)
    inverse_o[...] = jnp.broadcast_to(inverse, inverse_o.shape)
    normed = (value * inverse * gain[...].astype(jnp.float32)).astype(jnp.bfloat16)
    apg = (dot_t(gs[...], up[...]) * silu_slope(pre)).astype(jnp.bfloat16)
    apg_o[...] = apg
    carried = (gf[...].astype(jnp.float32) + dot(apg, down_t[...])).astype(jnp.bfloat16)
    for group in range(groups):

        @pl.when(rank == group)
        def _():
            part = slice(group * share, (group + 1) * share)
            lower_share[...] = lower[:, part]
            input_share[...] = (coupling * carried[:, part].astype(jnp.float32)).astype(
                jnp.bfloat16
            )

    for block in range(blocks):
        part = slice(block * column, (block + 1) * column)
        own = pl.multiple_of(place_of(block, me) * column, column)
        normed_own[:, pl.ds(own, column)] = normed[:, part]
        carried_own[:, pl.ds(own, column)] = carried[:, part]
        place = place_of(block, me ^ 4) * column - rank * share

        @pl.when((place >= 0) & (place < share))
        def _():
            first_send[:, pl.ds(pl.multiple_of(place, column), column)] = normed[:, part]

        @pl.when((place >= 0) & (place < share // 2))
        def _():
            to = pl.multiple_of(share + place, column)
            first_send[:, pl.ds(to, column)] = carried[:, part]

        @pl.when((place >= share // 2) & (place < share))
        def _():
            to = pl.multiple_of(place - share // 2, column)
            second_send[:, pl.ds(to, column)] = carried[:, part]


def head(at, blocks, groups, uf, us, gf, gs, gain, down_t, up):
    tokens, width = uf.shape
    rank = up.shape[0]
    share = width // groups
    step = 64 if tokens % 64 == 0 else tokens
    row = lambda columns: pl.BlockSpec((step, columns), lambda i: (i, 0))
    whole = lambda a: pl.BlockSpec(a.shape, lambda i: (0, 0))
    outs = [rank, rank, 128, width, share, share, width, width, share + share // 2, share // 2]
    types = [jnp.bfloat16, jnp.bfloat16, jnp.float32] + [jnp.bfloat16] * 7
    return call(
        functools.partial(head_body, blocks, groups),
        grid=(tokens // step,),
        in_specs=[SMEM] + [row(width)] * 4 + [whole(gain), whole(down_t), whole(up)],
        out_specs=[row(c) for c in outs],
        out_shape=[jax.ShapeDtypeStruct((tokens, c), t) for c, t in zip(outs, types)],
    )(at, uf, us, gf, gs, gain, down_t, up)


def both_body(at, own, part, other, out):
    tokens, share = part.shape
    out[:tokens] = own[...]
    for group in range(2):
        place = group * share

        @pl.when(at[1] == group)
        def _():
            out[tokens:, place : place + share] = part[...]
            out[tokens:, share - place : 2 * share - place] = other[...]


def both_tokens(at, own, part, other):
    tokens, width = own.shape
    return call(
        both_body,
        in_specs=[SMEM] + [pl.BlockSpec(memory_space=pltpu.VMEM)] * 3,
        out_specs=pl.BlockSpec(memory_space=pltpu.VMEM),
        out_shape=jax.ShapeDtypeStruct((2 * tokens, width), own.dtype),
    )(at, own, part, other)


def stack(*units):
    columns, dtype = units[0][0].shape[1], units[0][0].dtype
    arrays = []
    for array, _, _ in units:
        if not any(array is a for a in arrays):
            arrays.append(array)
    which = [next(k for k, a in enumerate(arrays) if a is u[0]) for u in units]
    total = sum(u[2] for u in units)

    def body(*refs):
        out, held, got, put = refs[-4:]
        reads, writes, at = [], [], 0
        for i, (_, first, rows) in enumerate(units):
            here = held.at[pl.ds(at, rows)]
            reads.append(
                pltpu.make_async_copy(refs[which[i]].at[pl.ds(first, rows)], here, got.at[i])
            )
            writes.append(pltpu.make_async_copy(here, out.at[pl.ds(at, rows)], put.at[i]))
            at += rows
        for read in reads:
            read.start()
        for read, write in zip(reads, writes):
            read.wait()
            write.start()
        for write in writes:
            write.wait()

    anywhere = pl.BlockSpec(memory_space=pl.ANY)
    return call(
        body,
        in_specs=[anywhere] * len(arrays),
        out_specs=anywhere,
        out_shape=jax.ShapeDtypeStruct((total, columns), dtype),
        scratch_shapes=[
            pltpu.VMEM((total, columns), dtype),
            pltpu.SemaphoreType.DMA((len(units),)),
            pltpu.SemaphoreType.DMA((len(units),)),
        ],
    )(*arrays)


ANY = pl.BlockSpec(memory_space=pl.ANY)


def fetch(units, refs, held, sems):
    copies, at = [], 0
    for i, (_, first, rows) in enumerate(units):
        copies.append(
            pltpu.make_async_copy(
                refs[i].at[pl.ds(first, rows)], held.at[pl.ds(at, rows)], sems.at[i]
            )
        )
        at += rows
    for copy in copies:
        copy.start()
    for copy in copies:
        copy.wait()


def held_scratch(units):
    array = units[0][0]
    return [
        pltpu.VMEM((sum(u[2] for u in units), array.shape[1]), array.dtype),
        pltpu.SemaphoreType.DMA((len(units),)),
    ]


def token_specs(count, width, step, at):
    half = count // step
    return [
        pl.BlockSpec((step, width), lambda i: (jnp.minimum(i, half - 1), at)),
        pl.BlockSpec((step, width), lambda i: (jnp.maximum(i - half, 0), at)),
    ]


def hidden_body(units, *refs):
    count = len(units)
    at, tokens, refs = refs[0], refs[1:7], refs[7:]
    hidden, slope, activated, held, sems = refs[count:]
    step = pl.program_id(0)

    @pl.when(step == 0)
    def _():
        fetch(units, refs, held, sems)

    def use(total):
        hidden[...] = total
        sigmoid_value = jax.nn.sigmoid(total)
        slope[...] = sigmoid_value * (1.0 + total * (1.0 - sigmoid_value))
        activated[...] = (total * sigmoid_value).astype(jnp.bfloat16)

    share = tokens[1].shape[1]
    for core in range(2):
        own, part, other = tokens[3 * core : 3 * core + 3]

        @pl.when(step == 2 * core)
        def _():
            use(dot(own[...], held[...]))

        for rank in range(2):

            @pl.when((step == 2 * core + 1) & (at[1] == rank))
            def _():
                first, second = (part, other) if rank == 0 else (other, part)
                use(dot(first[...], held[:share]) + dot(second[...], held[share:]))


def hidden_kernel(at, tokens, units):
    count = tokens[0].shape[0]
    columns = units[0][0].shape[1]
    out = pl.BlockSpec((count, columns), lambda i: (i, 0))
    return call(
        functools.partial(hidden_body, units),
        cost=work(8 * count * columns * tokens[0].shape[1]),
        room=56,
        grid=(4,),
        in_specs=[SMEM]
        + [pl.BlockSpec(t.shape, lambda i: (0, 0)) for t in tokens]
        + [ANY] * len(units),
        out_specs=[out] * 3,
        out_shape=[
            jax.ShapeDtypeStruct((4 * count, columns), t)
            for t in (jnp.float32, jnp.float32, jnp.bfloat16)
        ],
        scratch_shapes=held_scratch(units),
    )(at, *tokens, *[u[0] for u in units])


def act_body(units, places, depth, extras, slope_given, *refs):
    count = len(units)
    tokens, refs = refs[: 2 * places], refs[2 * places :]
    outs, (held, sems) = refs[count + extras : -2], refs[-2:]
    step = pl.program_id(0)

    @pl.when(step == 0)
    def _():
        fetch(units, refs, held, sems)

    cases = [(step == 0, 0), (step == 1, 0), (step >= 2, 1)]
    if not slope_given:
        cases = [(step < 2, 0), (step >= 2, 1)]
    for case, (chosen, which) in enumerate(cases):
        out = outs[case if slope_given else 0]

        @pl.when(chosen)
        def _():
            left = jnp.concatenate([t[...] for t in tokens[which::2]], axis=1)
            total = dot(left, held[...])
            if extras > slope_given:
                total = total + refs[count][...]
            if slope_given:
                total = total * refs[count + extras - 1][...]
            out[...] = total.astype(out.dtype)


def act_kernel(tokens, spans, partial, slope=None):
    count, width = tokens[0].shape
    units = [u for _, us in spans for u in us]
    depth = 2 * units[0][2]
    places = [
        first // depth + i for first, us in spans for i in range(sum(u[2] for u in us) // depth)
    ]
    columns = units[0][0].shape[1]
    step = count // 2
    out = pl.BlockSpec((step, columns), lambda i: (i, 0))
    extra = [a for a in (partial, slope) if a is not None]
    if slope is None:
        out_specs, out_shape = out, jax.ShapeDtypeStruct((2 * count, columns), jnp.float32)
    else:
        own = pl.BlockSpec((step, columns), lambda i: (0, 0))
        out_specs = [own, own, token_specs(count, columns, step, 0)[1]]
        out_shape = [
            jax.ShapeDtypeStruct((r, columns), jnp.bfloat16) for r in (step, step, count)
        ]
    return call(
        functools.partial(
            act_body, units, len(places), depth, len(extra), int(slope is not None)
        ),
        cost=work(4 * count * columns * depth * len(places)),
        room=36,
        grid=(4,),
        in_specs=sum([token_specs(count, depth, step, p) for p in places], [])
        + [ANY] * len(units)
        + [out] * len(extra),
        out_specs=out_specs,
        out_shape=out_shape,
        scratch_shapes=held_scratch(units),
    )(*[t for _ in places for t in tokens], *[u[0] for u in units], *extra)


def work(flops):
    return pl.CostEstimate(flops=flops // 4, bytes_accessed=0, transcendentals=0)


def parity_body(rows, quarter, eighth, at, weight, got, *refs):
    outs, (held, reads_done, writes_done) = refs[:2], refs[2:]
    core = at[0] & 1
    parity = (at[0] >> 2) & 1
    reads, writes = [], []
    for i in range(2):
        group = parity if i == 0 else 1 - parity
        for j, (source, base) in enumerate(((weight, core * quarter), (got, 0))):
            first = pl.multiple_of((core if j == 0 else 1 - core) * rows, rows)
            from_column = pl.multiple_of(base + group * eighth, 128)
            reads.append(
                pltpu.make_async_copy(
                    source.at[:, pl.ds(from_column, eighth)],
                    held.at[i, pl.ds(first, rows)],
                    reads_done.at[2 * i + j],
                )
            )
        writes.append(pltpu.make_async_copy(held.at[i], outs[i], writes_done.at[i]))
    for read in reads:
        read.start()
    for i in range(2):
        reads[2 * i].wait()
        reads[2 * i + 1].wait()
        writes[i].start()
    for write in writes:
        write.wait()


def parity_kernel(at, weight, got):
    rows, quarter = got.shape
    eighth = quarter // 2
    out = jax.ShapeDtypeStruct((2 * rows, eighth), weight.dtype)
    return call(
        functools.partial(parity_body, rows, quarter, eighth),
        in_specs=[SMEM, ANY, ANY],
        out_specs=[ANY, ANY],
        out_shape=[out, out],
        scratch_shapes=[
            pltpu.VMEM((2, 2 * rows, eighth), weight.dtype),
            pltpu.SemaphoreType.DMA((4,)),
            pltpu.SemaphoreType.DMA((2,)),
        ],
    )(at, weight, got)


def core_add_body(mine, got, own, partner):
    tokens = own.shape[0]
    total = mine[...] + got[...].astype(jnp.float32)
    own[...] = total[:tokens]
    partner[...] = total[tokens:].astype(jnp.bfloat16)


def core_add(mine, got):
    count, columns = mine.shape
    vmem = pl.BlockSpec(memory_space=pltpu.VMEM)
    return call(
        core_add_body,
        in_specs=[vmem, vmem],
        out_specs=[vmem, vmem],
        out_shape=[
            jax.ShapeDtypeStruct((count // 2, columns), jnp.float32),
            jax.ShapeDtypeStruct((count // 2, columns), jnp.bfloat16),
        ],
    )(mine, got)


def whole_add_body(mine, got, got_pair, own, partner):
    tokens = own.shape[0]
    total = mine[...] + got[...].astype(jnp.float32)
    own[...] = (total[:tokens] + got_pair[...].astype(jnp.float32)).astype(own.dtype)
    partner[...] = total[tokens:].astype(jnp.bfloat16)


def whole_add(mine, got, got_pair):
    count, columns = mine.shape
    vmem = pl.BlockSpec(memory_space=pltpu.VMEM)
    return call(
        whole_add_body,
        in_specs=[vmem] * 3,
        out_specs=[vmem, vmem],
        out_shape=[jax.ShapeDtypeStruct((count // 2, columns), jnp.bfloat16)] * 2,
    )(mine, got, got_pair)


def pair_add_body(swapped, own, got, out):
    half = own.shape[1] // 2
    if swapped:
        out[:, :half] = (own[:, :half] + got[:, half:].astype(jnp.float32)).astype(out.dtype)
        out[:, half:] = (own[:, half:] + got[:, :half].astype(jnp.float32)).astype(out.dtype)
    else:
        out[...] = (own[...] + got[...].astype(jnp.float32)).astype(out.dtype)


def pair_add(own, got, swapped=False):
    vmem = pl.BlockSpec(memory_space=pltpu.VMEM)
    return call(
        functools.partial(pair_add_body, swapped),
        in_specs=[vmem, vmem],
        out_specs=vmem,
        out_shape=jax.ShapeDtypeStruct(own.shape, jnp.bfloat16),
    )(own, got)


def out_body(units, left, *refs):
    own, other, held, sems = refs[len(units) :]
    step = pl.program_id(0)

    @pl.when(step == 0)
    def _():
        fetch(units, refs, held, sems)
        own[...] = dot_t(left[...], held[...])

    @pl.when(step == 1)
    def _():
        other[...] = dot_t(left[...], held[...]).astype(jnp.bfloat16)


def out_kernel(left, units):
    count, depth = left.shape
    columns = sum(u[2] for u in units)
    out = pl.BlockSpec((count // 2, columns), lambda i: (0, 0))
    return call(
        functools.partial(out_body, units),
        cost=work(2 * count * columns * depth),
        grid=(2,),
        in_specs=[pl.BlockSpec((count // 2, depth), lambda i: (i, 0))] + [ANY] * len(units),
        out_specs=[out, out],
        out_shape=[
            jax.ShapeDtypeStruct((count // 2, columns), jnp.float32),
            jax.ShapeDtypeStruct((count // 2, columns), jnp.bfloat16),
        ],
        scratch_shapes=held_scratch(units),
    )(left, *[u[0] for u in units])


def final_body(blocks, layers, at, gs, lower, gain, inverse, curvature, *refs):
    mine, got, out = refs[:layers], refs[layers:-1], refs[-1]
    me = at[0]
    width = out.shape[1]
    column = width // blocks
    scale = inverse[...][:, :1]
    drop = scale * scale * curvature[...] / width
    for place in range(blocks):
        layer, inner = divmod(place * column, mine[0].shape[1])
        part = slice(inner, inner + column)
        grad = mine[layer][:, part].astype(jnp.float32) + got[layer][:, part].astype(jnp.float32)
        spot = pl.ds(pl.multiple_of(block_at(place, me) * column, column), column)
        out[:, spot] = (
            gs[:, spot].astype(jnp.float32)
            + scale * gain[:, spot].astype(jnp.float32) * grad
            - lower[:, spot].astype(jnp.float32) * drop
        ).astype(jnp.bfloat16)


def final_kernel(at, blocks, gs, lower, gain, inverse, curvature, mine, got):
    tokens, width = gs.shape
    step = 64 if tokens % 64 == 0 else tokens
    row = lambda a: pl.BlockSpec((step, a.shape[1]), lambda i: (i, 0))
    return call(
        functools.partial(final_body, blocks, len(mine)),
        grid=(tokens // step,),
        in_specs=[SMEM, row(gs), row(lower), pl.BlockSpec(gain.shape, lambda i: (0, 0))]
        + [row(a) for a in [inverse, curvature, *mine, *got]],
        out_specs=row(gs),
        out_shape=jax.ShapeDtypeStruct(gs.shape, jnp.bfloat16),
    )(at, gs, lower, gain, inverse, curvature, *mine, *got)


def restore_body(blocks, layers, at, *refs):
    out = refs[layers]
    column = out.shape[1] // blocks
    for place in range(blocks):
        layer, inner = divmod(place * column, refs[0].shape[1])
        spot = pl.multiple_of(block_at(place, at[0]) * column, column)
        out[:, pl.ds(spot, column)] = refs[layer][:, inner : inner + column]


def restore(at, blocks, arrays):
    vmem = pl.BlockSpec(memory_space=pltpu.VMEM)
    tokens, chunk = arrays[0].shape
    return call(
        functools.partial(restore_body, blocks, len(arrays)),
        in_specs=[SMEM] + [vmem] * len(arrays),
        out_specs=vmem,
        out_shape=jax.ShapeDtypeStruct((tokens, chunk * len(arrays)), arrays[0].dtype),
    )(at, *arrays)


def first_body(blocks, at, upper, *refs):
    sums, got, out = refs[:4], refs[4:8], refs[8]
    me, rank = at[0], at[1]
    share = out.shape[1]
    chunk = share // 2
    column = 2 * share // blocks
    pair = (rank ^ (me >> 3)) & 1
    for which in range(2):

        @pl.when(pair == which)
        def _():
            for place in range(which * blocks // 2, (which + 1) * blocks // 2):
                layer, part = divmod(place * column, chunk)
                if which:
                    half, inner = divmod(part, chunk // 2)
                    layer, part = 2 + half, (layer - 2) * (chunk // 2) + inner
                block = block_at(place, me)
                to = pl.multiple_of(block * column - rank * share, column)
                columns = slice(part, part + column)
                frozen = sums[layer][:, columns].astype(jnp.float32) + got[layer][
                    :, columns
                ].astype(jnp.float32)
                out[:, pl.ds(to, column)] = (
                    (upper[:, pl.ds(to, column)].astype(jnp.float32) - frozen) / coupling
                ).astype(jnp.bfloat16)


def first_kernel(at, blocks, upper, sums, got):
    tokens, share = upper.shape
    step = 64 if tokens % 64 == 0 else tokens
    row = lambda columns: pl.BlockSpec((step, columns), lambda i: (i, 0))
    return call(
        functools.partial(first_body, blocks),
        grid=(tokens // step,),
        in_specs=[SMEM, row(share)] + [row(a.shape[1]) for a in [*sums, *got]],
        out_specs=row(share),
        out_shape=jax.ShapeDtypeStruct((tokens, share), jnp.bfloat16),
    )(at, upper, *sums, *got)


def on_device(
    upper_first,
    upper_second,
    grad_first,
    grad_second,
    norm_gain,
    up_weight,
    down_weight,
    adapter_down,
    adapter_up,
):
    size = lax.axis_size("dp")
    groups = lax.axis_size("mp")
    me = lax.axis_index("dp")
    mp_rank = lax.axis_index("mp")
    at = jnp.stack([me, mp_rank]).astype(jnp.int32)
    tokens, model_width = upper_first.shape
    layers = size // 4
    share_width = model_width // groups
    offset = mp_rank * share_width
    grad_scale = 1.0 / math.sqrt(tokens * size)
    parity = (me >> 2) & 1
    quarter = up_weight.shape[1] // 2
    gain = norm_gain.reshape(1, model_width)
    paired = groups == 2 and layers == 4

    rows = up_weight.shape[0]
    chunk = 4 * rows
    far = range(3, layers)
    eighth = quarter // 2
    core = me & 1

    def send_columns(weight):
        return lax.dynamic_slice_in_dim(weight, (1 - core) * quarter, quarter, 1)

    def by_parity(weight, got):
        if eighth % 128 == 0:
            return parity_kernel(at, weight, got)
        own = lax.dynamic_slice_in_dim(weight, core * quarter, quarter, 1)
        first = jnp.where(core == 0, own, got)
        pair = jnp.concatenate([first, jnp.where(core == 0, got, own)], axis=0)
        mine = lax.dynamic_slice_in_dim(pair, parity * eighth, eighth, 1)
        other = lax.dynamic_slice_in_dim(pair, (1 - parity) * eighth, eighth, 1)
        return [mine, other]

    def of_z(pair, s):
        return pair[s & 1]

    def units_of(piece, piece_y):
        return [(a, u * rows, rows) for u in range(2) for a in (piece, piece_y)]

    up_got = hop(send_columns(up_weight), 1)
    up = by_parity(up_weight, up_got)
    up, (down_weight, upper_first, upper_second, grad_first, grad_second, adapter_up) = together(
        up, (down_weight, upper_first, upper_second, grad_first, grad_second, adapter_up)
    )

    uz, uy, dz, dy = [[None] * layers for _ in range(4)]
    uz[0] = up[0]
    uz[2] = hop(up[0], 2 << 2)
    uz[1] = hop(up[1], 1 << 2)
    uy[0] = hop(up[0], 2)
    down = by_parity(down_weight, hop(send_columns(down_weight), 1))
    dz[0] = down[0]
    dy[0] = hop(down[0], 2)
    (
        squashed,
        adapter_pre_grad,
        inverse_rms,
        lower_full,
        lower_second,
        input_grad_first,
        normed_own,
        carried_own,
        first_send,
        second_send,
    ) = head(
        at,
        size,
        groups,
        upper_first,
        upper_second,
        grad_first,
        grad_second,
        gain,
        adapter_down.T,
        adapter_up,
    )
    up, down, uz, uy, dz, dy, normed_own, first_send, second_send, adapter_pre_grad, squashed = (
        together(
            up, down, uz, uy, dz, dy, normed_own, first_send, second_send, adapter_pre_grad,
            squashed,
        )
    )

    for s in far:
        uz[s] = hop(of_z(up, s), s << 2)
    first_part = hop(first_send, 4)
    uy[2] = hop(uz[2], 2)
    uy[1] = hop(uz[1], 2)
    sibling_own = hop(normed_own, 1)
    up_chunks = [stack(*units_of(uz[0], uy[0]))]
    upper_slice = lax.dynamic_slice_in_dim(upper_first, offset, share_width, 1)
    second_slice = lax.dynamic_slice_in_dim(grad_second, offset, share_width, 1)
    down_grad_part = (
        jnp.einsum("tr,td->rd", adapter_pre_grad, upper_slice, preferred_element_type=jnp.float32)
        * grad_scale
    )
    up_grad_part = (
        jnp.einsum("tr,td->rd", squashed, second_slice, preferred_element_type=jnp.float32)
        * grad_scale
    )
    rank = down_grad_part.shape[0]
    is_core, is_y = (me & 1) == 1, (me & 2) == 2
    keep = jnp.where(is_core, up_grad_part, down_grad_part)
    give = jnp.where(is_core, down_grad_part, up_grad_part).astype(jnp.bfloat16)
    normed_part = first_part[:, :share_width]
    uz, uy, normed_part, first_part, sibling_own, up_chunks, down, second_send, keep, give = (
        together(
            uz, uy, normed_part, first_part, sibling_own, up_chunks, down, second_send, keep, give
        )
    )

    low_rows, high_rows = slice(0, rows), slice(rows, 2 * rows)
    dzp = [[None, None] for _ in range(layers)]
    dyp = [[None, None] for _ in range(layers)]
    dzp[2][0] = hop(down[0][low_rows], 2 << 2)
    second_part = hop(second_send, 4)
    carried_part = jnp.concatenate([first_part[:, share_width:], second_part], axis=1)
    for s in far:
        uy[s] = hop(uz[s], 2)
    normed_other = swap_mp(normed_part) if groups == 2 else normed_part
    sibling_part = hop(normed_part, 1) if groups == 2 else normed_part
    up_chunks = up_chunks + [stack(*units_of(uz[s], uy[s])) for s in (1, 2)]
    downs = [[down[0][high_rows]], [down[1][low_rows]], [down[1][high_rows]]]
    (
        dzp, uz, uy, carried_part, normed_part, normed_other, sibling_own, sibling_part, downs,
        normed_own, carried_own, keep, give, up_chunks,
    ) = together(
        dzp, uz, uy, carried_part, normed_part, normed_other, sibling_own, sibling_part, downs,
        normed_own, carried_own, keep, give, up_chunks,
    )
    [mine_high], [other_low], [other_high] = downs

    for s in far:
        dzp[s][0] = hop(other_low if s & 1 else down[0][low_rows], s << 2)
    dzp[1][0] = hop(other_low, 1 << 2)
    dyp[2][0] = hop(dzp[2][0], 2)
    carried_other = swap_mp(carried_part) if groups == 2 else carried_part

    def pair_tokens(own, piece, other):
        if groups == 2:
            return both_tokens(at, own, piece, other)
        return jnp.concatenate([own, lax.all_gather(piece, "mp", axis=1, tiled=True)], axis=0)

    up_units = sum([units_of(uz[s], uy[s]) for s in range(layers)], [])
    if groups == 2:
        here = [normed_own, normed_part, normed_other]
        there = [sibling_own, sibling_part, hop(normed_other, 1)]
        rank_at = at
    else:
        whole = lax.all_gather(normed_part, "mp", axis=1, tiled=True)
        here = [normed_own, whole[:, : model_width // 2], whole[:, model_width // 2 :]]
        there = [hop(t, 1) for t in here]
        rank_at = at * jnp.array([1, 0], jnp.int32)
    hidden_pre, slope, activated = hidden_kernel(rank_at, here + there, up_units)
    (
        dzp, dyp, carried_part, carried_other, hidden_pre, slope, activated, mine_high, other_high,
        dz, dy, keep, give, uz, uy,
    ) = together(
        dzp, dyp, carried_part, carried_other, hidden_pre, slope, activated, mine_high, other_high,
        dz, dy, keep, give, uz, uy,
    )

    dzp[2][1] = hop(mine_high, 2 << 2)
    dzp[1][1] = hop(other_high, 1 << 2)
    for s in far:
        dyp[s][0] = hop(dzp[s][0], 2)
    dyp[1][0] = hop(dzp[1][0], 2)
    keep = keep + hop(give, 1).astype(jnp.float32)
    low, high = keep[: rank // 2], keep[rank // 2 :]
    share = jnp.where(is_y, high, low)
    give = jnp.where(is_y, low, high).astype(jnp.bfloat16)
    carried_both = pair_tokens(carried_own, carried_part, carried_other)
    zero = units_of(dz[0], dy[0])
    out_zero = out_kernel(activated, zero)
    up_chunks = up_chunks + [stack(*units_of(uz[s], uy[s])) for s in far]
    (
        dzp, dyp, carried_both, out_zero, share, give, mine_high, other_high, dz, dy, up_chunks,
    ) = together(
        dzp, dyp, carried_both, out_zero, share, give, mine_high, other_high, dz, dy, up_chunks
    )

    def unit(s, u):
        return [(dzp[s][u], 0, rows), (dyp[s][u], 0, rows)]

    zero = units_of(dz[0], dy[0])
    for s in far:
        dzp[s][1] = hop(other_high if s & 1 else mine_high, s << 2)
    dyp[2][1] = hop(dzp[2][1], 2)
    dyp[1][1] = hop(dzp[1][1], 2)
    carried_both = [carried_both, hop(carried_both, 1)]
    ends = range(2, layers)
    out_low = out_kernel(activated, sum([unit(s, 0) for s in ends], []))
    partial = act_kernel(
        carried_both,
        [(0, zero), (chunk, unit(1, 0))] + [(s * chunk, unit(s, 0)) for s in ends],
        None,
    )
    dzp, dyp, carried_both, out_zero, out_low, partial, slope, share, give = together(
        dzp, dyp, carried_both, out_zero, out_low, partial, slope, share, give
    )

    for s in far:
        dyp[s][1] = hop(dzp[s][1], 2)
    core_zero = core_add(out_zero[0], hop(out_zero[1], 1))
    got_one = hop(core_zero[1], 4)
    core_low = core_add(out_low[0], hop(out_low[1], 1))
    share = share + hop(give, 2).astype(jnp.float32)
    out_one = out_kernel(activated, unit(1, 0) + unit(1, 1))
    dyp, core_zero, got_one, core_low, out_one, share = together(
        dyp, core_zero, got_one, core_low, out_one, share
    )

    pre_own, pre_pair, pre_other = act_kernel(
        carried_both,
        [(s * chunk + chunk // 2, unit(s, 1)) for s in range(1, layers)],
        partial,
        slope,
    )

    def other_product(s):
        return dot_t(pre_other, up_chunks[s]).astype(jnp.bfloat16)

    def pair_product(s):
        return (
            dot_t(pre_pair, up_chunks[s]) + from_core[s][tokens:].astype(jnp.float32)
        ).astype(jnp.bfloat16)

    def own_product(s):
        return (
            dot_t(pre_own, up_chunks[s])
            + from_core[s][:tokens].astype(jnp.float32)
            + from_pair[s].astype(jnp.float32)
        ).astype(jnp.bfloat16)

    def share_mp(piece):
        if groups == 2:
            return swap_mp(piece)
        whole = lax.psum(piece.astype(jnp.float32), "mp")
        return whole - piece.astype(jnp.float32)

    to_core, from_core, to_pair, from_pair, grad_mine, grad_got = [
        [None] * layers for _ in range(6)
    ]
    to_core[0] = other_product(0)
    share = share + hop(share.astype(jnp.bfloat16), 4).astype(jnp.float32)
    got_low = hop(core_low[1], 4)
    one_got = hop(out_one[1], 1)
    (
        pre_own, pre_pair, pre_other, to_core, hidden_pre, share, activated, out_one, one_got,
        got_low, core_low,
    ) = together(
        pre_own, pre_pair, pre_other, to_core, hidden_pre, share, activated, out_one, one_got,
        got_low, core_low,
    )

    def to_holder(value, p):
        if not paired:
            return value
        moves = []
        for i in range(size):
            holder = ((i >> 3) ^ p) & 1
            moves.append((2 * i + 1 - holder, 2 * i + holder))
        return lax.ppermute(value, ("dp", "mp"), moves)

    from_core[0] = hop(to_core[0], 1)
    to_pair[0] = pair_product(0)
    to_core[1] = other_product(1)
    from_core, to_pair, to_core, pre_own, pre_pair, pre_other = together(
        from_core, to_pair, to_core, pre_own, pre_pair, pre_other
    )
    high, pair_one, core_high, got_zero, got_high = [None] * 5
    sum_one, sum_zero, sum_high, sent_zero, sent_one, sent_low, sent_high = [None] * 7
    stat = other = half = None
    for step in range(layers + 3):
        if step < layers:
            from_pair[step ^ 1] = hop(to_pair[step], 4)
        if 2 <= step < layers + 2:
            s = (step - 2) ^ 1
            grad_got[s] = share_mp(grad_mine[s])
        if 1 <= step <= layers:
            s = (step - 1) ^ 1
            grad_mine[s] = own_product(s)
        if step + 1 < layers:
            from_core[step + 1] = hop(to_core[step + 1], 1)
            to_pair[step + 1] = pair_product(step + 1)
        if step + 2 < layers:
            to_core[step + 2] = other_product(step + 2)
        if step == 0:
            sum_low = pair_add(core_low[0], got_low, swapped=True) if paired else None
            sum_one, pair_one = whole_add(out_one[0], one_got, got_one)
            stat = [
                jnp.sum(hidden_pre[first:last] * rows_of.astype(jnp.float32), axis=1)[:, None]
                for first, last, rows_of in (
                    (0, tokens, pre_own),
                    (tokens, 2 * tokens, pre_pair),
                    (2 * tokens, 4 * tokens, pre_other),
                )
            ]
        if step == 1:
            sent_one = to_holder(sum_one, 0)
            if paired:
                sent_low = to_holder(sum_low, 1)
            stat_got = hop(stat[2], 1)
            stat = [stat[0] + stat_got[:tokens], stat[1] + stat_got[tokens:]]
        if step == 2:
            high = out_kernel(activated, sum([unit(s, 1) for s in ends], []))
            stat = stat[0] + hop(stat[1], 4)
        if step == 3:
            core_high = core_add(high[0], hop(high[1], 1))
            stat = stat + swap_mp(stat) if groups == 2 else lax.psum(stat, "mp")
            bit = 8
            while bit < size:
                share = share + hop(share.astype(jnp.bfloat16), bit).astype(jnp.float32)
                bit *= 2
        if step == layers:
            got_zero = hop(pair_one, 4)
            other = hop(share, 2)
            half = jnp.concatenate(
                [jnp.where(is_y, other, share), jnp.where(is_y, share, other)], axis=0
            )
        if step == layers + 1:
            got_high = hop(core_high[1], 4)
            sum_zero = pair_add(core_zero[0], got_zero)
            other = hop(half, 1)
        if step == layers + 2:
            sent_zero = to_holder(sum_zero, 0)
            if paired:
                sum_high = pair_add(core_high[0], got_high, swapped=True)
                sent_high = to_holder(sum_high, 1)
            break
        state = (
            to_core, from_core, to_pair, from_pair, grad_mine, grad_got, high, pair_one, sum_low, core_high,
            got_zero, got_high, sum_one, sum_zero, sent_one, sent_low, stat, share, other, half,
            pre_own, pre_pair, pre_other, hidden_pre, activated, core_zero,
        )
        (
            to_core, from_core, to_pair, from_pair, grad_mine, grad_got, high, pair_one, sum_low, core_high,
            got_zero, got_high, sum_one, sum_zero, sent_one, sent_low, stat, share, other, half,
            pre_own, pre_pair, pre_other, hidden_pre, activated, core_zero,
        ) = together(*state)
    adapter_down_grad = jnp.where(is_core, other, half).T
    adapter_up_grad = jnp.where(is_core, half, other)

    input_grad_second = final_kernel(
        at, size, grad_second, lower_full, gain, inverse_rms, stat, grad_mine, grad_got
    )

    if paired:
        lower_first = first_kernel(
            at,
            size,
            upper_slice,
            [sum_zero, sum_one, sum_low, sum_high],
            [sent_zero, sent_one, sent_low, sent_high],
        )
    else:
        width = chunk // 2
        pieces = [sum_zero, sum_one]
        for s in ends:
            for own, got in ((core_low, got_low), (core_high, got_high)):
                mine = own[0][:, (s - 2) * width : (s - 1) * width]
                theirs = got[:, ((s ^ 1) - 2) * width : ((s ^ 1) - 1) * width]
                pieces.append((mine + theirs.astype(jnp.float32)).astype(jnp.bfloat16))
        chunks = pieces[:2] + [
            jnp.concatenate(pieces[i : i + 2], axis=1) for i in range(2, len(pieces), 2)
        ]
        out_whole = restore(at, size, chunks)
        frozen_share = lax.psum_scatter(
            out_whole.astype(jnp.float32), "mp", scatter_dimension=1, tiled=True
        )
        lower_first = ((upper_slice.astype(jnp.float32) - frozen_share) / coupling).astype(
            jnp.bfloat16
        )
    return (
        lower_first,
        lower_second,
        input_grad_first,
        input_grad_second,
        adapter_down_grad,
        adapter_up_grad,
    )


def solution(mesh):
    return jax.shard_map(
        on_device,
        mesh=mesh,
        in_specs=(
            P("dp", None),
            P("dp", None),
            P("dp", None),
            P("dp", None),
            P(),
            P("dp", "mp"),
            P("dp", "mp"),
            P(),
            P(),
        ),
        out_specs=(
            P("dp", "mp"),
            P("dp", "mp"),
            P("dp", "mp"),
            P("dp", None),
            P("mp", None),
            P(None, "mp"),
        ),
        check_vma=False,
    )
```

```python
import functools
import math

import jax
import jax.numpy as jnp
from jax import lax
from jax.experimental import pallas as pl
from jax.experimental.pallas import tpu as pltpu
from jax.sharding import PartitionSpec as P

coupling = 0.5
SMEM = pl.BlockSpec(memory_space=pltpu.SMEM)
FREE = pl.CostEstimate(flops=0, bytes_accessed=0, transcendentals=0)
MIB = 1024 * 1024


def silu_slope(argument):
    sigmoid_value = jax.nn.sigmoid(argument)
    return sigmoid_value * (1.0 + argument * (1.0 - sigmoid_value))


def after(value, *earlier):
    return lax.optimization_barrier((value, *earlier))[0]


def together(*values):
    return lax.optimization_barrier(values)


def hop(value, bits):
    size = lax.axis_size("dp")
    return lax.ppermute(value, "dp", [(i, i ^ bits) for i in range(size)])


def swap_mp(value):
    return lax.ppermute(value, "mp", [(0, 1), (1, 0)])


def place_of(block, me):
    relative = block ^ (me & ~1)
    return (relative & ~3) | ((relative & 1) << 1) | ((relative >> 1) & 1)


def block_at(place, me):
    return ((place & ~3) | ((place & 1) << 1) | ((place >> 1) & 1)) ^ (me & ~1)


def dot(left, right):
    return jnp.dot(left, right, preferred_element_type=jnp.float32)


def dot_t(left, right):
    return lax.dot_general(
        left, right, (((1,), (1,)), ((), ())), preferred_element_type=jnp.float32
    )


def call(body, cost=FREE, room=16, **settings):
    params = pltpu.CompilerParams(vmem_limit_bytes=room * MIB)
    return pl.pallas_call(body, compiler_params=params, cost_estimate=cost, **settings)


def head_body(blocks, groups, at, uf, us, gf, gs, gain, down_t, up, *outs):
    (squashed_o, apg_o, inverse_o, lower_o, lower_share, input_share) = outs[:6]
    normed_own, carried_own, first_send, second_send = outs[6:]
    me, rank = at[0], at[1]
    width = uf.shape[1]
    column = width // blocks
    share = width // groups
    pre = dot_t(uf[...], down_t[...])
    squashed = (pre * jax.nn.sigmoid(pre)).astype(jnp.bfloat16)
    squashed_o[...] = squashed
    lower = (us[...].astype(jnp.float32) - dot(squashed, up[...])).astype(jnp.bfloat16)
    lower_o[...] = lower
    value = lower.astype(jnp.float32)
    inverse = lax.rsqrt(jnp.mean(value * value, axis=1, keepdims=True) + 1e-05)
    inverse_o[...] = jnp.broadcast_to(inverse, inverse_o.shape)
    normed = (value * inverse * gain[...].astype(jnp.float32)).astype(jnp.bfloat16)
    apg = (dot_t(gs[...], up[...]) * silu_slope(pre)).astype(jnp.bfloat16)
    apg_o[...] = apg
    carried = (gf[...].astype(jnp.float32) + dot(apg, down_t[...])).astype(jnp.bfloat16)
    for group in range(groups):

        @pl.when(rank == group)
        def _():
            part = slice(group * share, (group + 1) * share)
            lower_share[...] = lower[:, part]
            input_share[...] = (coupling * carried[:, part].astype(jnp.float32)).astype(
                jnp.bfloat16
            )

    for block in range(blocks):
        part = slice(block * column, (block + 1) * column)
        own = pl.multiple_of(place_of(block, me) * column, column)
        normed_own[:, pl.ds(own, column)] = normed[:, part]
        carried_own[:, pl.ds(own, column)] = carried[:, part]
        place = place_of(block, me ^ 4) * column - rank * share

        @pl.when((place >= 0) & (place < share))
        def _():
            first_send[:, pl.ds(pl.multiple_of(place, column), column)] = normed[:, part]

        @pl.when((place >= 0) & (place < share // 2))
        def _():
            to = pl.multiple_of(share + place, column)
            first_send[:, pl.ds(to, column)] = carried[:, part]

        @pl.when((place >= share // 2) & (place < share))
        def _():
            to = pl.multiple_of(place - share // 2, column)
            second_send[:, pl.ds(to, column)] = carried[:, part]


def head(at, blocks, groups, uf, us, gf, gs, gain, down_t, up):
    tokens, width = uf.shape
    rank = up.shape[0]
    share = width // groups
    step = 64 if tokens % 64 == 0 else tokens
    row = lambda columns: pl.BlockSpec((step, columns), lambda i: (i, 0))
    whole = lambda a: pl.BlockSpec(a.shape, lambda i: (0, 0))
    outs = [rank, rank, 128, width, share, share, width, width, share + share // 2, share // 2]
    types = [jnp.bfloat16, jnp.bfloat16, jnp.float32] + [jnp.bfloat16] * 7
    return call(
        functools.partial(head_body, blocks, groups),
        grid=(tokens // step,),
        in_specs=[SMEM] + [row(width)] * 4 + [whole(gain), whole(down_t), whole(up)],
        out_specs=[row(c) for c in outs],
        out_shape=[jax.ShapeDtypeStruct((tokens, c), t) for c, t in zip(outs, types)],
    )(at, uf, us, gf, gs, gain, down_t, up)


def both_body(at, own, part, other, out):
    tokens, share = part.shape
    out[:tokens] = own[...]
    for group in range(2):
        place = group * share

        @pl.when(at[1] == group)
        def _():
            out[tokens:, place : place + share] = part[...]
            out[tokens:, share - place : 2 * share - place] = other[...]


def both_tokens(at, own, part, other):
    tokens, width = own.shape
    return call(
        both_body,
        in_specs=[SMEM] + [pl.BlockSpec(memory_space=pltpu.VMEM)] * 3,
        out_specs=pl.BlockSpec(memory_space=pltpu.VMEM),
        out_shape=jax.ShapeDtypeStruct((2 * tokens, width), own.dtype),
    )(at, own, part, other)


def stack(*units):
    columns, dtype = units[0][0].shape[1], units[0][0].dtype
    arrays = []
    for array, _, _ in units:
        if not any(array is a for a in arrays):
            arrays.append(array)
    which = [next(k for k, a in enumerate(arrays) if a is u[0]) for u in units]
    total = sum(u[2] for u in units)

    def body(*refs):
        out, held, got, put = refs[-4:]
        reads, writes, at = [], [], 0
        for i, (_, first, rows) in enumerate(units):
            here = held.at[pl.ds(at, rows)]
            reads.append(
                pltpu.make_async_copy(refs[which[i]].at[pl.ds(first, rows)], here, got.at[i])
            )
            writes.append(pltpu.make_async_copy(here, out.at[pl.ds(at, rows)], put.at[i]))
            at += rows
        for read in reads:
            read.start()
        for read, write in zip(reads, writes):
            read.wait()
            write.start()
        for write in writes:
            write.wait()

    anywhere = pl.BlockSpec(memory_space=pl.ANY)
    return call(
        body,
        in_specs=[anywhere] * len(arrays),
        out_specs=anywhere,
        out_shape=jax.ShapeDtypeStruct((total, columns), dtype),
        scratch_shapes=[
            pltpu.VMEM((total, columns), dtype),
            pltpu.SemaphoreType.DMA((len(units),)),
            pltpu.SemaphoreType.DMA((len(units),)),
        ],
    )(*arrays)


ANY = pl.BlockSpec(memory_space=pl.ANY)


def fetch(units, refs, held, sems):
    copies, at = [], 0
    for i, (_, first, rows) in enumerate(units):
        copies.append(
            pltpu.make_async_copy(
                refs[i].at[pl.ds(first, rows)], held.at[pl.ds(at, rows)], sems.at[i]
            )
        )
        at += rows
    for copy in copies:
        copy.start()
    for copy in copies:
        copy.wait()


def held_scratch(units):
    array = units[0][0]
    return [
        pltpu.VMEM((sum(u[2] for u in units), array.shape[1]), array.dtype),
        pltpu.SemaphoreType.DMA((len(units),)),
    ]


def token_specs(count, width, step, at):
    half = count // step
    return [
        pl.BlockSpec((step, width), lambda i: (jnp.minimum(i, half - 1), at)),
        pl.BlockSpec((step, width), lambda i: (jnp.maximum(i - half, 0), at)),
    ]


def hidden_body(units, *refs):
    count = len(units)
    at, tokens, refs = refs[0], refs[1:7], refs[7:]
    hidden, slope, activated, held, sems = refs[count:]
    step = pl.program_id(0)

    @pl.when(step == 0)
    def _():
        fetch(units, refs, held, sems)

    def use(total):
        hidden[...] = total
        sigmoid_value = jax.nn.sigmoid(total)
        slope[...] = sigmoid_value * (1.0 + total * (1.0 - sigmoid_value))
        activated[...] = (total * sigmoid_value).astype(jnp.bfloat16)

    share = tokens[1].shape[1]
    for core in range(2):
        own, part, other = tokens[3 * core : 3 * core + 3]

        @pl.when(step == 2 * core)
        def _():
            use(dot(own[...], held[...]))

        for rank in range(2):

            @pl.when((step == 2 * core + 1) & (at[1] == rank))
            def _():
                first, second = (part, other) if rank == 0 else (other, part)
                use(dot(first[...], held[:share]) + dot(second[...], held[share:]))


def hidden_kernel(at, tokens, units):
    count = tokens[0].shape[0]
    columns = units[0][0].shape[1]
    out = pl.BlockSpec((count, columns), lambda i: (i, 0))
    return call(
        functools.partial(hidden_body, units),
        cost=work(8 * count * columns * tokens[0].shape[1]),
        room=44,
        grid=(4,),
        in_specs=[SMEM]
        + [pl.BlockSpec(t.shape, lambda i: (0, 0)) for t in tokens]
        + [ANY] * len(units),
        out_specs=[out] * 3,
        out_shape=[
            jax.ShapeDtypeStruct((4 * count, columns), t)
            for t in (jnp.float32, jnp.float32, jnp.bfloat16)
        ],
        scratch_shapes=held_scratch(units),
    )(at, *tokens, *[u[0] for u in units])


def act_body(units, places, depth, extras, slope_given, *refs):
    count = len(units)
    tokens, refs = refs[: 2 * places], refs[2 * places :]
    outs, (held, sems) = refs[count + extras : -2], refs[-2:]
    step = pl.program_id(0)

    @pl.when(step == 0)
    def _():
        fetch(units, refs, held, sems)

    cases = [(step == 0, 0), (step == 1, 0), (step >= 2, 1)]
    if not slope_given:
        cases = [(step < 2, 0), (step >= 2, 1)]
    for case, (chosen, which) in enumerate(cases):
        out = outs[case if slope_given else 0]

        @pl.when(chosen)
        def _():
            left = jnp.concatenate([t[...] for t in tokens[which::2]], axis=1)
            total = dot(left, held[...])
            if extras > slope_given:
                total = total + refs[count][...]
            if slope_given:
                total = total * refs[count + extras - 1][...]
            out[...] = total.astype(out.dtype)


def act_kernel(tokens, spans, partial, slope=None):
    count, width = tokens[0].shape
    units = [u for _, us in spans for u in us]
    depth = 2 * units[0][2]
    places = [
        first // depth + i for first, us in spans for i in range(sum(u[2] for u in us) // depth)
    ]
    columns = units[0][0].shape[1]
    step = count // 2
    out = pl.BlockSpec((step, columns), lambda i: (i, 0))
    extra = [a for a in (partial, slope) if a is not None]
    if slope is None:
        out_specs, out_shape = out, jax.ShapeDtypeStruct((2 * count, columns), jnp.float32)
    else:
        own = pl.BlockSpec((step, columns), lambda i: (0, 0))
        out_specs = [own, own, token_specs(count, columns, step, 0)[1]]
        out_shape = [
            jax.ShapeDtypeStruct((r, columns), jnp.bfloat16) for r in (step, step, count)
        ]
    return call(
        functools.partial(
            act_body, units, len(places), depth, len(extra), int(slope is not None)
        ),
        cost=work(4 * count * columns * depth * len(places)),
        room=26,
        grid=(4,),
        in_specs=sum([token_specs(count, depth, step, p) for p in places], [])
        + [ANY] * len(units)
        + [out] * len(extra),
        out_specs=out_specs,
        out_shape=out_shape,
        scratch_shapes=held_scratch(units),
    )(*[t for _ in places for t in tokens], *[u[0] for u in units], *extra)


def work(flops):
    return pl.CostEstimate(flops=flops // 4, bytes_accessed=0, transcendentals=0)


def parity_body(rows, quarter, eighth, at, weight, got, *refs):
    outs, (held, reads_done, writes_done) = refs[:2], refs[2:]
    core = at[0] & 1
    parity = (at[0] >> 2) & 1
    reads, writes = [], []
    for i in range(2):
        group = parity if i == 0 else 1 - parity
        for j, (source, base) in enumerate(((weight, core * quarter), (got, 0))):
            first = pl.multiple_of((core if j == 0 else 1 - core) * rows, rows)
            from_column = pl.multiple_of(base + group * eighth, 128)
            reads.append(
                pltpu.make_async_copy(
                    source.at[:, pl.ds(from_column, eighth)],
                    held.at[i, pl.ds(first, rows)],
                    reads_done.at[2 * i + j],
                )
            )
        writes.append(pltpu.make_async_copy(held.at[i], outs[i], writes_done.at[i]))
    for read in reads:
        read.start()
    for i in range(2):
        reads[2 * i].wait()
        reads[2 * i + 1].wait()
        writes[i].start()
    for write in writes:
        write.wait()


def parity_kernel(at, weight, got):
    rows, quarter = got.shape
    eighth = quarter // 2
    out = jax.ShapeDtypeStruct((2 * rows, eighth), weight.dtype)
    return call(
        functools.partial(parity_body, rows, quarter, eighth),
        in_specs=[SMEM, ANY, ANY],
        out_specs=[ANY, ANY],
        out_shape=[out, out],
        scratch_shapes=[
            pltpu.VMEM((2, 2 * rows, eighth), weight.dtype),
            pltpu.SemaphoreType.DMA((4,)),
            pltpu.SemaphoreType.DMA((2,)),
        ],
    )(at, weight, got)


def core_add_body(mine, got, own, partner):
    tokens = own.shape[0]
    total = mine[...] + got[...].astype(jnp.float32)
    own[...] = total[:tokens]
    partner[...] = total[tokens:].astype(jnp.bfloat16)


def core_add(mine, got):
    count, columns = mine.shape
    vmem = pl.BlockSpec(memory_space=pltpu.VMEM)
    return call(
        core_add_body,
        in_specs=[vmem, vmem],
        out_specs=[vmem, vmem],
        out_shape=[
            jax.ShapeDtypeStruct((count // 2, columns), jnp.float32),
            jax.ShapeDtypeStruct((count // 2, columns), jnp.bfloat16),
        ],
    )(mine, got)


def whole_add_body(mine, got, got_pair, own, partner):
    tokens = own.shape[0]
    total = mine[...] + got[...].astype(jnp.float32)
    own[...] = (total[:tokens] + got_pair[...].astype(jnp.float32)).astype(own.dtype)
    partner[...] = total[tokens:].astype(jnp.bfloat16)


def whole_add(mine, got, got_pair):
    count, columns = mine.shape
    vmem = pl.BlockSpec(memory_space=pltpu.VMEM)
    return call(
        whole_add_body,
        in_specs=[vmem] * 3,
        out_specs=[vmem, vmem],
        out_shape=[jax.ShapeDtypeStruct((count // 2, columns), jnp.bfloat16)] * 2,
    )(mine, got, got_pair)


def pair_add_body(swapped, own, got, out):
    half = own.shape[1] // 2
    if swapped:
        out[:, :half] = (own[:, :half] + got[:, half:].astype(jnp.float32)).astype(out.dtype)
        out[:, half:] = (own[:, half:] + got[:, :half].astype(jnp.float32)).astype(out.dtype)
    else:
        out[...] = (own[...] + got[...].astype(jnp.float32)).astype(out.dtype)


def pair_add(own, got, swapped=False):
    vmem = pl.BlockSpec(memory_space=pltpu.VMEM)
    return call(
        functools.partial(pair_add_body, swapped),
        in_specs=[vmem, vmem],
        out_specs=vmem,
        out_shape=jax.ShapeDtypeStruct(own.shape, jnp.bfloat16),
    )(own, got)


def out_body(units, left, *refs):
    own, other, held, sems = refs[len(units) :]
    step = pl.program_id(0)

    @pl.when(step == 0)
    def _():
        fetch(units, refs, held, sems)
        own[...] = dot_t(left[...], held[...])

    @pl.when(step == 1)
    def _():
        other[...] = dot_t(left[...], held[...]).astype(jnp.bfloat16)


def out_kernel(left, units):
    count, depth = left.shape
    columns = sum(u[2] for u in units)
    out = pl.BlockSpec((count // 2, columns), lambda i: (0, 0))
    return call(
        functools.partial(out_body, units),
        cost=work(2 * count * columns * depth),
        grid=(2,),
        in_specs=[pl.BlockSpec((count // 2, depth), lambda i: (i, 0))] + [ANY] * len(units),
        out_specs=[out, out],
        out_shape=[
            jax.ShapeDtypeStruct((count // 2, columns), jnp.float32),
            jax.ShapeDtypeStruct((count // 2, columns), jnp.bfloat16),
        ],
        scratch_shapes=held_scratch(units),
    )(left, *[u[0] for u in units])


def final_body(blocks, layers, at, gs, lower, gain, inverse, curvature, *refs):
    mine, got, out = refs[:layers], refs[layers:-1], refs[-1]
    me = at[0]
    width = out.shape[1]
    column = width // blocks
    scale = inverse[...][:, :1]
    drop = scale * scale * curvature[...] / width
    for place in range(blocks):
        layer, inner = divmod(place * column, mine[0].shape[1])
        part = slice(inner, inner + column)
        grad = mine[layer][:, part].astype(jnp.float32) + got[layer][:, part].astype(jnp.float32)
        spot = pl.ds(pl.multiple_of(block_at(place, me) * column, column), column)
        out[:, spot] = (
            gs[:, spot].astype(jnp.float32)
            + scale * gain[:, spot].astype(jnp.float32) * grad
            - lower[:, spot].astype(jnp.float32) * drop
        ).astype(jnp.bfloat16)


def final_kernel(at, blocks, gs, lower, gain, inverse, curvature, mine, got):
    tokens, width = gs.shape
    step = 64 if tokens % 64 == 0 else tokens
    row = lambda a: pl.BlockSpec((step, a.shape[1]), lambda i: (i, 0))
    return call(
        functools.partial(final_body, blocks, len(mine)),
        grid=(tokens // step,),
        in_specs=[SMEM, row(gs), row(lower), pl.BlockSpec(gain.shape, lambda i: (0, 0))]
        + [row(a) for a in [inverse, curvature, *mine, *got]],
        out_specs=row(gs),
        out_shape=jax.ShapeDtypeStruct(gs.shape, jnp.bfloat16),
    )(at, gs, lower, gain, inverse, curvature, *mine, *got)


def restore_body(blocks, layers, at, *refs):
    out = refs[layers]
    column = out.shape[1] // blocks
    for place in range(blocks):
        layer, inner = divmod(place * column, refs[0].shape[1])
        spot = pl.multiple_of(block_at(place, at[0]) * column, column)
        out[:, pl.ds(spot, column)] = refs[layer][:, inner : inner + column]


def restore(at, blocks, arrays):
    vmem = pl.BlockSpec(memory_space=pltpu.VMEM)
    tokens, chunk = arrays[0].shape
    return call(
        functools.partial(restore_body, blocks, len(arrays)),
        in_specs=[SMEM] + [vmem] * len(arrays),
        out_specs=vmem,
        out_shape=jax.ShapeDtypeStruct((tokens, chunk * len(arrays)), arrays[0].dtype),
    )(at, *arrays)


def first_body(blocks, at, upper, *refs):
    sums, got, out = refs[:4], (refs[5], refs[4], refs[4], refs[5]), refs[6]
    me, rank = at[0], at[1]
    share = out.shape[1]
    chunk = share // 2
    column = 2 * share // blocks
    pair = (rank ^ (me >> 3)) & 1
    for which in range(2):

        @pl.when(pair == which)
        def _():
            for place in range(which * blocks // 2, (which + 1) * blocks // 2):
                layer, part = divmod(place * column, chunk)
                if which:
                    half, inner = divmod(part, chunk // 2)
                    layer, part = 2 + half, (layer - 2) * (chunk // 2) + inner
                block = block_at(place, me)
                to = pl.multiple_of(block * column - rank * share, column)
                columns = slice(part, part + column)
                frozen = sums[layer][:, columns].astype(jnp.float32) + got[layer][
                    :, columns
                ].astype(jnp.float32)
                out[:, pl.ds(to, column)] = (
                    (upper[:, pl.ds(to, column)].astype(jnp.float32) - frozen) / coupling
                ).astype(jnp.bfloat16)


def first_kernel(at, blocks, upper, sums, got):
    tokens, share = upper.shape
    step = 64 if tokens % 64 == 0 else tokens
    row = lambda columns: pl.BlockSpec((step, columns), lambda i: (i, 0))
    return call(
        functools.partial(first_body, blocks),
        grid=(tokens // step,),
        in_specs=[SMEM, row(share)] + [row(a.shape[1]) for a in [*sums, *got]],
        out_specs=row(share),
        out_shape=jax.ShapeDtypeStruct((tokens, share), jnp.bfloat16),
    )(at, upper, *sums, *got)


def on_device(
    upper_first,
    upper_second,
    grad_first,
    grad_second,
    norm_gain,
    up_weight,
    down_weight,
    adapter_down,
    adapter_up,
):
    size = lax.axis_size("dp")
    groups = lax.axis_size("mp")
    me = lax.axis_index("dp")
    mp_rank = lax.axis_index("mp")
    at = jnp.stack([me, mp_rank]).astype(jnp.int32)
    tokens, model_width = upper_first.shape
    layers = size // 4
    share_width = model_width // groups
    offset = mp_rank * share_width
    grad_scale = 1.0 / math.sqrt(tokens * size)
    parity = (me >> 2) & 1
    quarter = up_weight.shape[1] // 2
    gain = norm_gain.reshape(1, model_width)
    paired = groups == 2 and layers == 4

    rows = up_weight.shape[0]
    chunk = 4 * rows
    far = range(3, layers)
    eighth = quarter // 2
    core = me & 1

    def send_columns(weight):
        return lax.dynamic_slice_in_dim(weight, (1 - core) * quarter, quarter, 1)

    def by_parity(weight, got):
        if eighth % 128 == 0:
            return parity_kernel(at, weight, got)
        own = lax.dynamic_slice_in_dim(weight, core * quarter, quarter, 1)
        first = jnp.where(core == 0, own, got)
        pair = jnp.concatenate([first, jnp.where(core == 0, got, own)], axis=0)
        mine = lax.dynamic_slice_in_dim(pair, parity * eighth, eighth, 1)
        other = lax.dynamic_slice_in_dim(pair, (1 - parity) * eighth, eighth, 1)
        return [mine, other]

    def of_z(pair, s):
        return pair[s & 1]

    def units_of(piece, piece_y):
        return [(a, u * rows, rows) for u in range(2) for a in (piece, piece_y)]

    up_got = hop(send_columns(up_weight), 1)
    up = by_parity(up_weight, up_got)
    up, (down_weight, upper_first, upper_second, grad_first, grad_second, adapter_up) = together(
        up, (down_weight, upper_first, upper_second, grad_first, grad_second, adapter_up)
    )

    uz, uy, dz, dy = [[None] * layers for _ in range(4)]
    uz[0] = up[0]
    uz[2] = hop(up[0], 2 << 2)
    uz[1] = hop(up[1], 1 << 2)
    uy[0] = hop(up[0], 2)
    down = by_parity(down_weight, hop(send_columns(down_weight), 1))
    dz[0] = down[0]
    dy[0] = hop(down[0], 2)
    low_rows, high_rows = slice(0, rows), slice(rows, 2 * rows)
    down_parts = [[d[part] for part in (low_rows, high_rows)] for d in down]
    (
        squashed,
        adapter_pre_grad,
        inverse_rms,
        lower_full,
        lower_second,
        input_grad_first,
        normed_own,
        carried_own,
        first_send,
        second_send,
    ) = head(
        at,
        size,
        groups,
        upper_first,
        upper_second,
        grad_first,
        grad_second,
        gain,
        adapter_down.T,
        adapter_up,
    )
    (
        up, down_parts, uz, uy, dz, dy, normed_own, first_send, second_send, adapter_pre_grad,
        squashed,
    ) = together(
        up, down_parts, uz, uy, dz, dy, normed_own, first_send, second_send, adapter_pre_grad,
        squashed,
    )

    for s in far:
        uz[s] = hop(of_z(up, s), s << 2)
    first_part = hop(first_send, 4)
    uy[2] = hop(uz[2], 2)
    uy[1] = hop(uz[1], 2)
    sibling_own = hop(normed_own, 1)
    up_chunks = [stack(*units_of(uz[0], uy[0]))]
    upper_slice = lax.dynamic_slice_in_dim(upper_first, offset, share_width, 1)
    second_slice = lax.dynamic_slice_in_dim(grad_second, offset, share_width, 1)
    down_grad_part = (
        jnp.einsum("tr,td->rd", adapter_pre_grad, upper_slice, preferred_element_type=jnp.float32)
        * grad_scale
    )
    up_grad_part = (
        jnp.einsum("tr,td->rd", squashed, second_slice, preferred_element_type=jnp.float32)
        * grad_scale
    )
    rank = down_grad_part.shape[0]
    is_core, is_y = (me & 1) == 1, (me & 2) == 2
    keep = jnp.where(is_core, up_grad_part, down_grad_part)
    give = jnp.where(is_core, down_grad_part, up_grad_part).astype(jnp.bfloat16)
    normed_part = first_part[:, :share_width]
    (
        uz, uy, normed_part, first_part, sibling_own, up_chunks, down_parts, second_send, keep,
        give,
    ) = together(
        uz, uy, normed_part, first_part, sibling_own, up_chunks, down_parts, second_send, keep,
        give,
    )

    dzp = [[None, None] for _ in range(layers)]
    dyp = [[None, None] for _ in range(layers)]
    dzp[2][0] = hop(down_parts[0][0], 2 << 2)
    second_part = hop(second_send, 4)
    carried_part = jnp.concatenate([first_part[:, share_width:], second_part], axis=1)
    for s in far:
        uy[s] = hop(uz[s], 2)
    normed_other = swap_mp(normed_part) if groups == 2 else normed_part
    sibling_part = hop(normed_part, 1) if groups == 2 else normed_part
    up_chunks = up_chunks + [stack(*units_of(uz[s], uy[s])) for s in (1, 2)]
    (
        dzp, uz, uy, carried_part, normed_part, normed_other, sibling_own, sibling_part, down_parts,
        normed_own, carried_own, keep, give, up_chunks,
    ) = together(
        dzp, uz, uy, carried_part, normed_part, normed_other, sibling_own, sibling_part, down_parts,
        normed_own, carried_own, keep, give, up_chunks,
    )
    (mine_low, mine_high), (other_low, other_high) = down_parts

    for s in far:
        dzp[s][0] = hop(other_low if s & 1 else mine_low, s << 2)
    dzp[1][0] = hop(other_low, 1 << 2)
    dyp[2][0] = hop(dzp[2][0], 2)
    carried_other = swap_mp(carried_part) if groups == 2 else carried_part

    def pair_tokens(own, piece, other):
        if groups == 2:
            return both_tokens(at, own, piece, other)
        return jnp.concatenate([own, lax.all_gather(piece, "mp", axis=1, tiled=True)], axis=0)

    up_units = sum([units_of(uz[s], uy[s]) for s in range(layers)], [])
    if groups == 2:
        here = [normed_own, normed_part, normed_other]
        there = [sibling_own, sibling_part, hop(normed_other, 1)]
        rank_at = at
    else:
        whole = lax.all_gather(normed_part, "mp", axis=1, tiled=True)
        here = [normed_own, whole[:, : model_width // 2], whole[:, model_width // 2 :]]
        there = [hop(t, 1) for t in here]
        rank_at = at * jnp.array([1, 0], jnp.int32)
    hidden_pre, slope, activated = hidden_kernel(rank_at, here + there, up_units)
    (
        dzp, dyp, carried_part, carried_other, hidden_pre, slope, activated, mine_high, other_high,
        dz, dy, keep, give, uz, uy,
    ) = together(
        dzp, dyp, carried_part, carried_other, hidden_pre, slope, activated, mine_high, other_high,
        dz, dy, keep, give, uz, uy,
    )

    dzp[2][1] = hop(mine_high, 2 << 2)
    dzp[1][1] = hop(other_high, 1 << 2)
    for s in far:
        dyp[s][0] = hop(dzp[s][0], 2)
    dyp[1][0] = hop(dzp[1][0], 2)
    keep = keep + hop(give, 1).astype(jnp.float32)
    low, high = keep[: rank // 2], keep[rank // 2 :]
    share = jnp.where(is_y, high, low)
    give = jnp.where(is_y, low, high).astype(jnp.bfloat16)
    carried_both = pair_tokens(carried_own, carried_part, carried_other)
    zero = units_of(dz[0], dy[0])
    out_zero = out_kernel(activated, zero)
    up_chunks = up_chunks + [stack(*units_of(uz[s], uy[s])) for s in far]
    (
        dzp, dyp, carried_both, out_zero, share, give, mine_high, other_high, dz, dy, up_chunks,
    ) = together(
        dzp, dyp, carried_both, out_zero, share, give, mine_high, other_high, dz, dy, up_chunks
    )

    def unit(s, u):
        return [(dzp[s][u], 0, rows), (dyp[s][u], 0, rows)]

    zero = units_of(dz[0], dy[0])
    for s in far:
        dzp[s][1] = hop(other_high if s & 1 else mine_high, s << 2)
    dyp[2][1] = hop(dzp[2][1], 2)
    dyp[1][1] = hop(dzp[1][1], 2)
    carried_both = [carried_both, hop(carried_both, 1)]
    ends = range(2, layers)
    out_low = out_kernel(activated, sum([unit(s, 0) for s in ends], []))
    partial = act_kernel(
        carried_both,
        [(0, zero), (chunk, unit(1, 0))] + [(s * chunk, unit(s, 0)) for s in ends],
        None,
    )
    dzp, dyp, carried_both, out_zero, out_low, partial, slope, share, give = together(
        dzp, dyp, carried_both, out_zero, out_low, partial, slope, share, give
    )

    for s in far:
        dyp[s][1] = hop(dzp[s][1], 2)
    core_zero = core_add(out_zero[0], hop(out_zero[1], 1))
    got_one = hop(core_zero[1], 4)
    core_low = core_add(out_low[0], hop(out_low[1], 1))
    share = share + hop(give, 2).astype(jnp.float32)
    out_one = out_kernel(activated, unit(1, 0) + unit(1, 1))
    dyp, core_zero, got_one, core_low, out_one, share = together(
        dyp, core_zero, got_one, core_low, out_one, share
    )

    pre_own, pre_pair, pre_other = act_kernel(
        carried_both,
        [(s * chunk + chunk // 2, unit(s, 1)) for s in range(1, layers)],
        partial,
        slope,
    )

    def other_product(s):
        return dot_t(pre_other, up_chunks[s]).astype(jnp.bfloat16)

    def pair_product(s):
        return (
            dot_t(pre_pair, up_chunks[s]) + from_core[s][tokens:].astype(jnp.float32)
        ).astype(jnp.bfloat16)

    def own_product(s):
        return (
            dot_t(pre_own, up_chunks[s])
            + from_core[s][:tokens].astype(jnp.float32)
            + from_pair[s].astype(jnp.float32)
        ).astype(jnp.bfloat16)

    def share_mp(piece):
        if groups == 2:
            return swap_mp(piece)
        whole = lax.psum(piece.astype(jnp.float32), "mp")
        return whole - piece.astype(jnp.float32)

    to_core, from_core, to_pair, from_pair, grad_mine, grad_got = [
        [None] * layers for _ in range(6)
    ]
    to_core[0] = other_product(0)
    share = share + hop(share.astype(jnp.bfloat16), 4).astype(jnp.float32)
    got_low = hop(core_low[1], 4)
    one_got = hop(out_one[1], 1)
    (
        pre_own, pre_pair, pre_other, to_core, hidden_pre, share, activated, out_one, one_got,
        got_low, core_low,
    ) = together(
        pre_own, pre_pair, pre_other, to_core, hidden_pre, share, activated, out_one, one_got,
        got_low, core_low,
    )

    holds_low = ((mp_rank ^ (me >> 3)) & 1) == 0

    def swap_held(low, high):
        return swap_mp(jnp.where(holds_low, high, low))

    from_core[0] = hop(to_core[0], 1)
    to_pair[0] = pair_product(0)
    to_core[1] = other_product(1)
    from_core, to_pair, to_core, pre_own, pre_pair, pre_other = together(
        from_core, to_pair, to_core, pre_own, pre_pair, pre_other
    )
    high, pair_one, core_high, got_zero, got_high = [None] * 5
    sum_one, sum_zero, sum_high, sent_zero, sent_one = [None] * 5
    stat = other = half = None
    for step in range(layers + 3):
        if step < layers:
            from_pair[step ^ 1] = hop(to_pair[step], 4)
        if 2 <= step < layers + 2:
            s = (step - 2) ^ 1
            grad_got[s] = share_mp(grad_mine[s])
        if 1 <= step <= layers:
            s = (step - 1) ^ 1
            grad_mine[s] = own_product(s)
        if step + 1 < layers:
            from_core[step + 1] = hop(to_core[step + 1], 1)
            to_pair[step + 1] = pair_product(step + 1)
        if step + 2 < layers:
            to_core[step + 2] = other_product(step + 2)
        if step == 0:
            sum_low = pair_add(core_low[0], got_low, swapped=True) if paired else None
            sum_one, pair_one = whole_add(out_one[0], one_got, got_one)
            stat = [
                jnp.sum(hidden_pre[first:last] * rows_of.astype(jnp.float32), axis=1)[:, None]
                for first, last, rows_of in (
                    (0, tokens, pre_own),
                    (tokens, 2 * tokens, pre_pair),
                    (2 * tokens, 4 * tokens, pre_other),
                )
            ]
        if step == 1:
            if paired:
                sent_one = swap_held(sum_one, sum_low)
            stat_got = hop(stat[2], 1)
            stat = [stat[0] + stat_got[:tokens], stat[1] + stat_got[tokens:]]
        if step == 2:
            high = out_kernel(activated, sum([unit(s, 1) for s in ends], []))
            stat = stat[0] + hop(stat[1], 4)
        if step == 3:
            core_high = core_add(high[0], hop(high[1], 1))
            stat = stat + swap_mp(stat) if groups == 2 else lax.psum(stat, "mp")
            bit = 8
            while bit < size:
                share = share + hop(share.astype(jnp.bfloat16), bit).astype(jnp.float32)
                bit *= 2
        if step == layers:
            got_zero = hop(pair_one, 4)
            other = hop(share, 2)
            half = jnp.concatenate(
                [jnp.where(is_y, other, share), jnp.where(is_y, share, other)], axis=0
            )
        if step == layers + 1:
            got_high = hop(core_high[1], 4)
            sum_zero = pair_add(core_zero[0], got_zero)
            other = hop(half, 1)
        if step == layers + 2:
            if paired:
                sum_high = pair_add(core_high[0], got_high, swapped=True)
                sent_zero = swap_held(sum_zero, sum_high)
            break
        state = (
            to_core, from_core, to_pair, from_pair, grad_mine, grad_got, high, pair_one, sum_low, core_high,
            got_zero, got_high, sum_one, sum_zero, sent_one, stat, share, other, half,
            pre_own, pre_pair, pre_other, hidden_pre, activated, core_zero,
        )
        (
            to_core, from_core, to_pair, from_pair, grad_mine, grad_got, high, pair_one, sum_low, core_high,
            got_zero, got_high, sum_one, sum_zero, sent_one, stat, share, other, half,
            pre_own, pre_pair, pre_other, hidden_pre, activated, core_zero,
        ) = together(*state)
    adapter_down_grad = jnp.where(is_core, other, half).T
    adapter_up_grad = jnp.where(is_core, half, other)

    input_grad_second = final_kernel(
        at, size, grad_second, lower_full, gain, inverse_rms, stat, grad_mine, grad_got
    )

    if paired:
        lower_first = first_kernel(
            at,
            size,
            upper_slice,
            [sum_zero, sum_one, sum_low, sum_high],
            [sent_one, sent_zero],
        )
    else:
        width = chunk // 2
        pieces = [sum_zero, sum_one]
        for s in ends:
            for own, got in ((core_low, got_low), (core_high, got_high)):
                mine = own[0][:, (s - 2) * width : (s - 1) * width]
                theirs = got[:, ((s ^ 1) - 2) * width : ((s ^ 1) - 1) * width]
                pieces.append((mine + theirs.astype(jnp.float32)).astype(jnp.bfloat16))
        chunks = pieces[:2] + [
            jnp.concatenate(pieces[i : i + 2], axis=1) for i in range(2, len(pieces), 2)
        ]
        out_whole = restore(at, size, chunks)
        frozen_share = lax.psum_scatter(
            out_whole.astype(jnp.float32), "mp", scatter_dimension=1, tiled=True
        )
        lower_first = ((upper_slice.astype(jnp.float32) - frozen_share) / coupling).astype(
            jnp.bfloat16
        )
    return (
        lower_first,
        lower_second,
        input_grad_first,
        input_grad_second,
        adapter_down_grad,
        adapter_up_grad,
    )


def solution(mesh):
    return jax.shard_map(
        on_device,
        mesh=mesh,
        in_specs=(
            P("dp", None),
            P("dp", None),
            P("dp", None),
            P("dp", None),
            P(),
            P("dp", "mp"),
            P("dp", "mp"),
            P(),
            P(),
        ),
        out_specs=(
            P("dp", "mp"),
            P("dp", "mp"),
            P("dp", "mp"),
            P("dp", None),
            P("mp", None),
            P(None, "mp"),
        ),
        check_vma=False,
    )
```

```python
import functools
import math

import jax
import jax.numpy as jnp
from jax import lax
from jax.experimental import pallas as pl
from jax.experimental.pallas import tpu as pltpu
from jax.sharding import PartitionSpec as P

coupling = 0.5
SMEM = pl.BlockSpec(memory_space=pltpu.SMEM)
FREE = pl.CostEstimate(flops=0, bytes_accessed=0, transcendentals=0)
MIB = 1024 * 1024


def silu_slope(argument):
    sigmoid_value = jax.nn.sigmoid(argument)
    return sigmoid_value * (1.0 + argument * (1.0 - sigmoid_value))


def after(value, *earlier):
    return lax.optimization_barrier((value, *earlier))[0]


def together(*values):
    return lax.optimization_barrier(values)


def hop(value, bits):
    size = lax.axis_size("dp")
    return lax.ppermute(value, "dp", [(i, i ^ bits) for i in range(size)])


def swap_mp(value):
    return lax.ppermute(value, "mp", [(0, 1), (1, 0)])


def place_of(block, me):
    relative = block ^ (me & ~1)
    return (relative & ~3) | ((relative & 1) << 1) | ((relative >> 1) & 1)


def block_at(place, me):
    return ((place & ~3) | ((place & 1) << 1) | ((place >> 1) & 1)) ^ (me & ~1)


def dot(left, right):
    return jnp.dot(left, right, preferred_element_type=jnp.float32)


def dot_t(left, right):
    return lax.dot_general(
        left, right, (((1,), (1,)), ((), ())), preferred_element_type=jnp.float32
    )


def call(body, cost=FREE, room=16, **settings):
    params = pltpu.CompilerParams(vmem_limit_bytes=room * MIB)
    return pl.pallas_call(body, compiler_params=params, cost_estimate=cost, **settings)


def head_body(blocks, groups, at, uf, us, gf, gs, gain, down_t, up, *outs):
    (squashed_o, apg_o, inverse_o, lower_o, lower_share, input_share) = outs[:6]
    normed_own, carried_own, first_send, second_send = outs[6:]
    me, rank = at[0], at[1]
    width = uf.shape[1]
    column = width // blocks
    share = width // groups
    pre = dot_t(uf[...], down_t[...])
    squashed = (pre * jax.nn.sigmoid(pre)).astype(jnp.bfloat16)
    squashed_o[...] = squashed
    lower = (us[...].astype(jnp.float32) - dot(squashed, up[...])).astype(jnp.bfloat16)
    lower_o[...] = lower
    value = lower.astype(jnp.float32)
    inverse = lax.rsqrt(jnp.mean(value * value, axis=1, keepdims=True) + 1e-05)
    inverse_o[...] = jnp.broadcast_to(inverse, inverse_o.shape)
    normed = (value * inverse * gain[...].astype(jnp.float32)).astype(jnp.bfloat16)
    apg = (dot_t(gs[...], up[...]) * silu_slope(pre)).astype(jnp.bfloat16)
    apg_o[...] = apg
    carried = (gf[...].astype(jnp.float32) + dot(apg, down_t[...])).astype(jnp.bfloat16)
    for group in range(groups):

        @pl.when(rank == group)
        def _():
            part = slice(group * share, (group + 1) * share)
            lower_share[...] = lower[:, part]
            input_share[...] = (coupling * carried[:, part].astype(jnp.float32)).astype(
                jnp.bfloat16
            )

    for block in range(blocks):
        part = slice(block * column, (block + 1) * column)
        own = pl.multiple_of(place_of(block, me) * column, column)
        normed_own[:, pl.ds(own, column)] = normed[:, part]
        carried_own[:, pl.ds(own, column)] = carried[:, part]
        place = place_of(block, me ^ 4) * column - rank * share

        @pl.when((place >= 0) & (place < share))
        def _():
            first_send[:, pl.ds(pl.multiple_of(place, column), column)] = normed[:, part]

        @pl.when((place >= 0) & (place < share // 2))
        def _():
            to = pl.multiple_of(share + place, column)
            first_send[:, pl.ds(to, column)] = carried[:, part]

        @pl.when((place >= share // 2) & (place < share))
        def _():
            to = pl.multiple_of(place - share // 2, column)
            second_send[:, pl.ds(to, column)] = carried[:, part]


def head(at, blocks, groups, uf, us, gf, gs, gain, down_t, up):
    tokens, width = uf.shape
    rank = up.shape[0]
    share = width // groups
    step = 64 if tokens % 64 == 0 else tokens
    row = lambda columns: pl.BlockSpec((step, columns), lambda i: (i, 0))
    whole = lambda a: pl.BlockSpec(a.shape, lambda i: (0, 0))
    outs = [rank, rank, 128, width, share, share, width, width, share + share // 2, share // 2]
    types = [jnp.bfloat16, jnp.bfloat16, jnp.float32] + [jnp.bfloat16] * 7
    return call(
        functools.partial(head_body, blocks, groups),
        grid=(tokens // step,),
        in_specs=[SMEM] + [row(width)] * 4 + [whole(gain), whole(down_t), whole(up)],
        out_specs=[row(c) for c in outs],
        out_shape=[jax.ShapeDtypeStruct((tokens, c), t) for c, t in zip(outs, types)],
    )(at, uf, us, gf, gs, gain, down_t, up)


def both_body(at, own, part, other, out):
    tokens, share = part.shape
    out[:tokens] = own[...]
    for group in range(2):
        place = group * share

        @pl.when(at[1] == group)
        def _():
            out[tokens:, place : place + share] = part[...]
            out[tokens:, share - place : 2 * share - place] = other[...]


def both_tokens(at, own, part, other):
    tokens, width = own.shape
    return call(
        both_body,
        in_specs=[SMEM] + [pl.BlockSpec(memory_space=pltpu.VMEM)] * 3,
        out_specs=pl.BlockSpec(memory_space=pltpu.VMEM),
        out_shape=jax.ShapeDtypeStruct((2 * tokens, width), own.dtype),
    )(at, own, part, other)


def stack(*units):
    columns, dtype = units[0][0].shape[1], units[0][0].dtype
    arrays = []
    for array, _, _ in units:
        if not any(array is a for a in arrays):
            arrays.append(array)
    which = [next(k for k, a in enumerate(arrays) if a is u[0]) for u in units]
    total = sum(u[2] for u in units)

    def body(*refs):
        out, held, got, put = refs[-4:]
        reads, writes, at = [], [], 0
        for i, (_, first, rows) in enumerate(units):
            here = held.at[pl.ds(at, rows)]
            reads.append(
                pltpu.make_async_copy(refs[which[i]].at[pl.ds(first, rows)], here, got.at[i])
            )
            writes.append(pltpu.make_async_copy(here, out.at[pl.ds(at, rows)], put.at[i]))
            at += rows
        for read in reads:
            read.start()
        for read, write in zip(reads, writes):
            read.wait()
            write.start()
        for write in writes:
            write.wait()

    anywhere = pl.BlockSpec(memory_space=pl.ANY)
    return call(
        body,
        in_specs=[anywhere] * len(arrays),
        out_specs=anywhere,
        out_shape=jax.ShapeDtypeStruct((total, columns), dtype),
        scratch_shapes=[
            pltpu.VMEM((total, columns), dtype),
            pltpu.SemaphoreType.DMA((len(units),)),
            pltpu.SemaphoreType.DMA((len(units),)),
        ],
    )(*arrays)


ANY = pl.BlockSpec(memory_space=pl.ANY)


def fetch(units, refs, held, sems):
    copies, at = [], 0
    for i, (_, first, rows) in enumerate(units):
        copies.append(
            pltpu.make_async_copy(
                refs[i].at[pl.ds(first, rows)], held.at[pl.ds(at, rows)], sems.at[i]
            )
        )
        at += rows
    for copy in copies:
        copy.start()
    for copy in copies:
        copy.wait()


def held_scratch(units):
    array = units[0][0]
    return [
        pltpu.VMEM((sum(u[2] for u in units), array.shape[1]), array.dtype),
        pltpu.SemaphoreType.DMA((len(units),)),
    ]


def token_specs(count, width, step, at):
    half = count // step
    return [
        pl.BlockSpec((step, width), lambda i: (jnp.minimum(i, half - 1), at)),
        pl.BlockSpec((step, width), lambda i: (jnp.maximum(i - half, 0), at)),
    ]


def hidden_body(units, *refs):
    count = len(units)
    at, tokens, refs = refs[0], refs[1:7], refs[7:]
    hidden, slope, activated, held, sems = refs[count:]
    step = pl.program_id(0)

    @pl.when(step == 0)
    def _():
        fetch(units, refs, held, sems)

    def use(total):
        hidden[...] = total
        sigmoid_value = jax.nn.sigmoid(total)
        slope[...] = sigmoid_value * (1.0 + total * (1.0 - sigmoid_value))
        activated[...] = (total * sigmoid_value).astype(jnp.bfloat16)

    share = tokens[1].shape[1]
    for core in range(2):
        own, part, other = tokens[3 * core : 3 * core + 3]

        @pl.when(step == 2 * core)
        def _():
            use(dot(own[...], held[...]))

        for rank in range(2):

            @pl.when((step == 2 * core + 1) & (at[1] == rank))
            def _():
                first, second = (part, other) if rank == 0 else (other, part)
                use(dot(first[...], held[:share]) + dot(second[...], held[share:]))


def hidden_kernel(at, tokens, units):
    count = tokens[0].shape[0]
    columns = units[0][0].shape[1]
    out = pl.BlockSpec((count, columns), lambda i: (i, 0))
    return call(
        functools.partial(hidden_body, units),
        cost=work(8 * count * columns * tokens[0].shape[1]),
        room=44,
        grid=(4,),
        in_specs=[SMEM]
        + [pl.BlockSpec(t.shape, lambda i: (0, 0)) for t in tokens]
        + [ANY] * len(units),
        out_specs=[out] * 3,
        out_shape=[
            jax.ShapeDtypeStruct((4 * count, columns), t)
            for t in (jnp.float32, jnp.float32, jnp.bfloat16)
        ],
        scratch_shapes=held_scratch(units),
    )(at, *tokens, *[u[0] for u in units])


def act_body(units, places, depth, extras, slope_given, *refs):
    count = len(units)
    tokens, refs = refs[: 2 * places], refs[2 * places :]
    outs, (held, sems) = refs[count + extras : -2], refs[-2:]
    step = pl.program_id(0)

    @pl.when(step == 0)
    def _():
        fetch(units, refs, held, sems)

    cases = [(step == 0, 0), (step == 1, 0), (step >= 2, 1)]
    if not slope_given:
        cases = [(step < 2, 0), (step >= 2, 1)]
    for case, (chosen, which) in enumerate(cases):
        out = outs[case if slope_given else 0]

        @pl.when(chosen)
        def _():
            left = jnp.concatenate([t[...] for t in tokens[which::2]], axis=1)
            total = dot(left, held[...])
            if extras:
                total = total + refs[count][...]
            if slope_given:
                total = total * refs[count + 1][...]
            rounded = total.astype(out.dtype)
            out[...] = rounded
            if slope_given:
                product = refs[count + 2][...] * rounded.astype(jnp.float32)
                outs[-1][...] = jnp.sum(product, axis=1, keepdims=True)


def act_kernel(tokens, spans, partial, slope=None, hidden=None):
    count, width = tokens[0].shape
    units = [u for _, us in spans for u in us]
    depth = 2 * units[0][2]
    places = [
        first // depth + i for first, us in spans for i in range(sum(u[2] for u in us) // depth)
    ]
    columns = units[0][0].shape[1]
    step = count // 2
    out = pl.BlockSpec((step, columns), lambda i: (i, 0))
    extra = [a for a in (partial, slope, hidden) if a is not None]
    if slope is None:
        out_specs, out_shape = out, jax.ShapeDtypeStruct((2 * count, columns), jnp.float32)
    else:
        own = pl.BlockSpec((step, columns), lambda i: (0, 0))
        out_specs = [own, own, token_specs(count, columns, step, 0)[1]]
        out_specs.append(pl.BlockSpec((step, 1), lambda i: (i, 0)))
        out_shape = [
            jax.ShapeDtypeStruct((r, columns), jnp.bfloat16) for r in (step, step, count)
        ]
        out_shape.append(jax.ShapeDtypeStruct((2 * count, 1), jnp.float32))
    return call(
        functools.partial(
            act_body, units, len(places), depth, len(extra), int(slope is not None)
        ),
        cost=work(4 * count * columns * depth * len(places)),
        room=26,
        grid=(4,),
        in_specs=sum([token_specs(count, depth, step, p) for p in places], [])
        + [ANY] * len(units)
        + [out] * len(extra),
        out_specs=out_specs,
        out_shape=out_shape,
        scratch_shapes=held_scratch(units),
    )(*[t for _ in places for t in tokens], *[u[0] for u in units], *extra)


def work(flops):
    return pl.CostEstimate(flops=flops // 4, bytes_accessed=0, transcendentals=0)


def parity_body(rows, quarter, eighth, at, weight, got, *refs):
    outs, (held, reads_done, writes_done) = refs[:2], refs[2:]
    core = at[0] & 1
    parity = (at[0] >> 2) & 1
    reads, writes = [], []
    for i in range(2):
        group = parity if i == 0 else 1 - parity
        for j, (source, base) in enumerate(((weight, core * quarter), (got, 0))):
            first = pl.multiple_of((core if j == 0 else 1 - core) * rows, rows)
            from_column = pl.multiple_of(base + group * eighth, 128)
            reads.append(
                pltpu.make_async_copy(
                    source.at[:, pl.ds(from_column, eighth)],
                    held.at[i, pl.ds(first, rows)],
                    reads_done.at[2 * i + j],
                )
            )
        writes.append(pltpu.make_async_copy(held.at[i], outs[i], writes_done.at[i]))
    for read in reads:
        read.start()
    for i in range(2):
        reads[2 * i].wait()
        reads[2 * i + 1].wait()
        writes[i].start()
    for write in writes:
        write.wait()


def parity_kernel(at, weight, got):
    rows, quarter = got.shape
    eighth = quarter // 2
    out = jax.ShapeDtypeStruct((2 * rows, eighth), weight.dtype)
    return call(
        functools.partial(parity_body, rows, quarter, eighth),
        in_specs=[SMEM, ANY, ANY],
        out_specs=[ANY, ANY],
        out_shape=[out, out],
        scratch_shapes=[
            pltpu.VMEM((2, 2 * rows, eighth), weight.dtype),
            pltpu.SemaphoreType.DMA((4,)),
            pltpu.SemaphoreType.DMA((2,)),
        ],
    )(at, weight, got)


def core_add_body(mine, got, own, partner):
    tokens = own.shape[0]
    total = mine[...] + got[...].astype(jnp.float32)
    own[...] = total[:tokens]
    partner[...] = total[tokens:].astype(jnp.bfloat16)


def core_add(mine, got):
    count, columns = mine.shape
    vmem = pl.BlockSpec(memory_space=pltpu.VMEM)
    return call(
        core_add_body,
        in_specs=[vmem, vmem],
        out_specs=[vmem, vmem],
        out_shape=[
            jax.ShapeDtypeStruct((count // 2, columns), jnp.float32),
            jax.ShapeDtypeStruct((count // 2, columns), jnp.bfloat16),
        ],
    )(mine, got)


def whole_add_body(mine, got, got_pair, own, partner):
    tokens = own.shape[0]
    total = mine[...] + got[...].astype(jnp.float32)
    own[...] = (total[:tokens] + got_pair[...].astype(jnp.float32)).astype(own.dtype)
    partner[...] = total[tokens:].astype(jnp.bfloat16)


def whole_add(mine, got, got_pair):
    count, columns = mine.shape
    vmem = pl.BlockSpec(memory_space=pltpu.VMEM)
    return call(
        whole_add_body,
        in_specs=[vmem] * 3,
        out_specs=[vmem, vmem],
        out_shape=[jax.ShapeDtypeStruct((count // 2, columns), jnp.bfloat16)] * 2,
    )(mine, got, got_pair)


def pair_add_body(swapped, own, got, out):
    half = own.shape[1] // 2
    if swapped:
        out[:, :half] = (own[:, :half] + got[:, half:].astype(jnp.float32)).astype(out.dtype)
        out[:, half:] = (own[:, half:] + got[:, :half].astype(jnp.float32)).astype(out.dtype)
    else:
        out[...] = (own[...] + got[...].astype(jnp.float32)).astype(out.dtype)


def pair_add(own, got, swapped=False):
    vmem = pl.BlockSpec(memory_space=pltpu.VMEM)
    return call(
        functools.partial(pair_add_body, swapped),
        in_specs=[vmem, vmem],
        out_specs=vmem,
        out_shape=jax.ShapeDtypeStruct(own.shape, jnp.bfloat16),
    )(own, got)


def out_body(units, left, *refs):
    own, other, held, sems = refs[len(units) :]
    step = pl.program_id(0)

    @pl.when(step == 0)
    def _():
        fetch(units, refs, held, sems)
        own[...] = dot_t(left[...], held[...])

    @pl.when(step == 1)
    def _():
        other[...] = dot_t(left[...], held[...]).astype(jnp.bfloat16)


def out_kernel(left, units):
    count, depth = left.shape
    columns = sum(u[2] for u in units)
    out = pl.BlockSpec((count // 2, columns), lambda i: (0, 0))
    return call(
        functools.partial(out_body, units),
        cost=work(2 * count * columns * depth),
        grid=(2,),
        in_specs=[pl.BlockSpec((count // 2, depth), lambda i: (i, 0))] + [ANY] * len(units),
        out_specs=[out, out],
        out_shape=[
            jax.ShapeDtypeStruct((count // 2, columns), jnp.float32),
            jax.ShapeDtypeStruct((count // 2, columns), jnp.bfloat16),
        ],
        scratch_shapes=held_scratch(units),
    )(left, *[u[0] for u in units])


def final_body(blocks, layers, at, gs, lower, gain, inverse, curvature, *refs):
    mine, got, out = refs[:layers], refs[layers:-1], refs[-1]
    me = at[0]
    width = out.shape[1]
    column = width // blocks
    scale = inverse[...][:, :1]
    drop = scale * scale * curvature[...] / width
    for place in range(blocks):
        layer, inner = divmod(place * column, mine[0].shape[1])
        part = slice(inner, inner + column)
        grad = mine[layer][:, part].astype(jnp.float32) + got[layer][:, part].astype(jnp.float32)
        spot = pl.ds(pl.multiple_of(block_at(place, me) * column, column), column)
        out[:, spot] = (
            gs[:, spot].astype(jnp.float32)
            + scale * gain[:, spot].astype(jnp.float32) * grad
            - lower[:, spot].astype(jnp.float32) * drop
        ).astype(jnp.bfloat16)


def final_kernel(at, blocks, gs, lower, gain, inverse, curvature, mine, got):
    tokens, width = gs.shape
    step = 64 if tokens % 64 == 0 else tokens
    row = lambda a: pl.BlockSpec((step, a.shape[1]), lambda i: (i, 0))
    return call(
        functools.partial(final_body, blocks, len(mine)),
        grid=(tokens // step,),
        in_specs=[SMEM, row(gs), row(lower), pl.BlockSpec(gain.shape, lambda i: (0, 0))]
        + [row(a) for a in [inverse, curvature, *mine, *got]],
        out_specs=row(gs),
        out_shape=jax.ShapeDtypeStruct(gs.shape, jnp.bfloat16),
    )(at, gs, lower, gain, inverse, curvature, *mine, *got)


def restore_body(blocks, layers, at, *refs):
    out = refs[layers]
    column = out.shape[1] // blocks
    for place in range(blocks):
        layer, inner = divmod(place * column, refs[0].shape[1])
        spot = pl.multiple_of(block_at(place, at[0]) * column, column)
        out[:, pl.ds(spot, column)] = refs[layer][:, inner : inner + column]


def restore(at, blocks, arrays):
    vmem = pl.BlockSpec(memory_space=pltpu.VMEM)
    tokens, chunk = arrays[0].shape
    return call(
        functools.partial(restore_body, blocks, len(arrays)),
        in_specs=[SMEM] + [vmem] * len(arrays),
        out_specs=vmem,
        out_shape=jax.ShapeDtypeStruct((tokens, chunk * len(arrays)), arrays[0].dtype),
    )(at, *arrays)


def first_body(blocks, at, upper, *refs):
    sums, got, out = refs[:4], (refs[5], refs[4], refs[4], refs[5]), refs[6]
    me, rank = at[0], at[1]
    share = out.shape[1]
    chunk = share // 2
    column = 2 * share // blocks
    pair = (rank ^ (me >> 3)) & 1
    for which in range(2):

        @pl.when(pair == which)
        def _():
            for place in range(which * blocks // 2, (which + 1) * blocks // 2):
                layer, part = divmod(place * column, chunk)
                if which:
                    half, inner = divmod(part, chunk // 2)
                    layer, part = 2 + half, (layer - 2) * (chunk // 2) + inner
                block = block_at(place, me)
                to = pl.multiple_of(block * column - rank * share, column)
                columns = slice(part, part + column)
                frozen = sums[layer][:, columns].astype(jnp.float32) + got[layer][
                    :, columns
                ].astype(jnp.float32)
                out[:, pl.ds(to, column)] = (
                    (upper[:, pl.ds(to, column)].astype(jnp.float32) - frozen) / coupling
                ).astype(jnp.bfloat16)


def first_kernel(at, blocks, upper, sums, got):
    tokens, share = upper.shape
    step = 64 if tokens % 64 == 0 else tokens
    row = lambda columns: pl.BlockSpec((step, columns), lambda i: (i, 0))
    return call(
        functools.partial(first_body, blocks),
        grid=(tokens // step,),
        in_specs=[SMEM, row(share)] + [row(a.shape[1]) for a in [*sums, *got]],
        out_specs=row(share),
        out_shape=jax.ShapeDtypeStruct((tokens, share), jnp.bfloat16),
    )(at, upper, *sums, *got)


def on_device(
    upper_first,
    upper_second,
    grad_first,
    grad_second,
    norm_gain,
    up_weight,
    down_weight,
    adapter_down,
    adapter_up,
):
    size = lax.axis_size("dp")
    groups = lax.axis_size("mp")
    me = lax.axis_index("dp")
    mp_rank = lax.axis_index("mp")
    at = jnp.stack([me, mp_rank]).astype(jnp.int32)
    tokens, model_width = upper_first.shape
    layers = size // 4
    share_width = model_width // groups
    offset = mp_rank * share_width
    grad_scale = 1.0 / math.sqrt(tokens * size)
    parity = (me >> 2) & 1
    quarter = up_weight.shape[1] // 2
    gain = norm_gain.reshape(1, model_width)
    paired = groups == 2 and layers == 4

    rows = up_weight.shape[0]
    chunk = 4 * rows
    far = range(3, layers)
    eighth = quarter // 2
    core = me & 1

    def send_columns(weight):
        return lax.dynamic_slice_in_dim(weight, (1 - core) * quarter, quarter, 1)

    def by_parity(weight, got):
        if eighth % 128 == 0:
            return parity_kernel(at, weight, got)
        own = lax.dynamic_slice_in_dim(weight, core * quarter, quarter, 1)
        first = jnp.where(core == 0, own, got)
        pair = jnp.concatenate([first, jnp.where(core == 0, got, own)], axis=0)
        mine = lax.dynamic_slice_in_dim(pair, parity * eighth, eighth, 1)
        other = lax.dynamic_slice_in_dim(pair, (1 - parity) * eighth, eighth, 1)
        return [mine, other]

    def of_z(pair, s):
        return pair[s & 1]

    def units_of(piece, piece_y):
        return [(a, u * rows, rows) for u in range(2) for a in (piece, piece_y)]

    up_got = hop(send_columns(up_weight), 1)
    up = by_parity(up_weight, up_got)
    up, (down_weight, upper_first, upper_second, grad_first, grad_second, adapter_up) = together(
        up, (down_weight, upper_first, upper_second, grad_first, grad_second, adapter_up)
    )

    uz, uy, dz, dy = [[None] * layers for _ in range(4)]
    uz[0] = up[0]
    uz[2] = hop(up[0], 2 << 2)
    uz[1] = hop(up[1], 1 << 2)
    uy[0] = hop(up[0], 2)
    down = by_parity(down_weight, hop(send_columns(down_weight), 1))
    dz[0] = down[0]
    dy[0] = hop(down[0], 2)
    low_rows, high_rows = slice(0, rows), slice(rows, 2 * rows)
    down_parts = [[d[part] for part in (low_rows, high_rows)] for d in down]
    (
        squashed,
        adapter_pre_grad,
        inverse_rms,
        lower_full,
        lower_second,
        input_grad_first,
        normed_own,
        carried_own,
        first_send,
        second_send,
    ) = head(
        at,
        size,
        groups,
        upper_first,
        upper_second,
        grad_first,
        grad_second,
        gain,
        adapter_down.T,
        adapter_up,
    )
    (
        up, down_parts, uz, uy, dz, dy, normed_own, first_send, second_send, adapter_pre_grad,
        squashed,
    ) = together(
        up, down_parts, uz, uy, dz, dy, normed_own, first_send, second_send, adapter_pre_grad,
        squashed,
    )

    for s in far:
        uz[s] = hop(of_z(up, s), s << 2)
    first_part = hop(first_send, 4)
    uy[2] = hop(uz[2], 2)
    uy[1] = hop(uz[1], 2)
    sibling_own = hop(normed_own, 1)
    up_chunks = [stack(*units_of(uz[0], uy[0]))]
    upper_slice = lax.dynamic_slice_in_dim(upper_first, offset, share_width, 1)
    second_slice = lax.dynamic_slice_in_dim(grad_second, offset, share_width, 1)
    down_grad_part = (
        jnp.einsum("tr,td->rd", adapter_pre_grad, upper_slice, preferred_element_type=jnp.float32)
        * grad_scale
    )
    up_grad_part = (
        jnp.einsum("tr,td->rd", squashed, second_slice, preferred_element_type=jnp.float32)
        * grad_scale
    )
    rank = down_grad_part.shape[0]
    is_core, is_y = (me & 1) == 1, (me & 2) == 2
    keep = jnp.where(is_core, up_grad_part, down_grad_part)
    give = jnp.where(is_core, down_grad_part, up_grad_part).astype(jnp.bfloat16)
    normed_part = first_part[:, :share_width]
    (
        uz, uy, normed_part, first_part, sibling_own, up_chunks, down_parts, second_send, keep,
        give,
    ) = together(
        uz, uy, normed_part, first_part, sibling_own, up_chunks, down_parts, second_send, keep,
        give,
    )

    dzp = [[None, None] for _ in range(layers)]
    dyp = [[None, None] for _ in range(layers)]
    dzp[2][0] = hop(down_parts[0][0], 2 << 2)
    second_part = hop(second_send, 4)
    carried_part = jnp.concatenate([first_part[:, share_width:], second_part], axis=1)
    for s in far:
        uy[s] = hop(uz[s], 2)
    normed_other = swap_mp(normed_part) if groups == 2 else normed_part
    sibling_part = hop(normed_part, 1) if groups == 2 else normed_part
    up_chunks = up_chunks + [stack(*units_of(uz[s], uy[s])) for s in (1, 2)]
    (
        dzp, uz, uy, carried_part, normed_part, normed_other, sibling_own, sibling_part, down_parts,
        normed_own, carried_own, keep, give, up_chunks,
    ) = together(
        dzp, uz, uy, carried_part, normed_part, normed_other, sibling_own, sibling_part, down_parts,
        normed_own, carried_own, keep, give, up_chunks,
    )
    (mine_low, mine_high), (other_low, other_high) = down_parts

    for s in far:
        dzp[s][0] = hop(other_low if s & 1 else mine_low, s << 2)
    dzp[1][0] = hop(other_low, 1 << 2)
    dyp[2][0] = hop(dzp[2][0], 2)
    carried_other = swap_mp(carried_part) if groups == 2 else carried_part

    def pair_tokens(own, piece, other):
        if groups == 2:
            return both_tokens(at, own, piece, other)
        return jnp.concatenate([own, lax.all_gather(piece, "mp", axis=1, tiled=True)], axis=0)

    up_units = sum([units_of(uz[s], uy[s]) for s in range(layers)], [])
    if groups == 2:
        here = [normed_own, normed_part, normed_other]
        there = [sibling_own, sibling_part, hop(normed_other, 1)]
        rank_at = at
    else:
        whole = lax.all_gather(normed_part, "mp", axis=1, tiled=True)
        here = [normed_own, whole[:, : model_width // 2], whole[:, model_width // 2 :]]
        there = [hop(t, 1) for t in here]
        rank_at = at * jnp.array([1, 0], jnp.int32)
    hidden_pre, slope, activated = hidden_kernel(rank_at, here + there, up_units)
    (
        dzp, dyp, carried_part, carried_other, hidden_pre, slope, activated, mine_high, other_high,
        dz, dy, keep, give, uz, uy,
    ) = together(
        dzp, dyp, carried_part, carried_other, hidden_pre, slope, activated, mine_high, other_high,
        dz, dy, keep, give, uz, uy,
    )

    dzp[2][1] = hop(mine_high, 2 << 2)
    dzp[1][1] = hop(other_high, 1 << 2)
    for s in far:
        dyp[s][0] = hop(dzp[s][0], 2)
    dyp[1][0] = hop(dzp[1][0], 2)
    keep = keep + hop(give, 1).astype(jnp.float32)
    low, high = keep[: rank // 2], keep[rank // 2 :]
    share = jnp.where(is_y, high, low)
    give = jnp.where(is_y, low, high).astype(jnp.bfloat16)
    carried_both = pair_tokens(carried_own, carried_part, carried_other)
    zero = units_of(dz[0], dy[0])
    out_zero = out_kernel(activated, zero)
    up_chunks = up_chunks + [stack(*units_of(uz[s], uy[s])) for s in far]
    (
        dzp, dyp, carried_both, out_zero, share, give, mine_high, other_high, dz, dy, up_chunks,
    ) = together(
        dzp, dyp, carried_both, out_zero, share, give, mine_high, other_high, dz, dy, up_chunks
    )

    def unit(s, u):
        return [(dzp[s][u], 0, rows), (dyp[s][u], 0, rows)]

    zero = units_of(dz[0], dy[0])
    for s in far:
        dzp[s][1] = hop(other_high if s & 1 else mine_high, s << 2)
    dyp[2][1] = hop(dzp[2][1], 2)
    dyp[1][1] = hop(dzp[1][1], 2)
    carried_both = [carried_both, hop(carried_both, 1)]
    ends = range(2, layers)
    out_low = out_kernel(activated, sum([unit(s, 0) for s in ends], []))
    partial = act_kernel(
        carried_both,
        [(0, zero), (chunk, unit(1, 0))] + [(s * chunk, unit(s, 0)) for s in ends],
        None,
    )
    dzp, dyp, carried_both, out_zero, out_low, partial, slope, share, give = together(
        dzp, dyp, carried_both, out_zero, out_low, partial, slope, share, give
    )

    for s in far:
        dyp[s][1] = hop(dzp[s][1], 2)
    core_zero = core_add(out_zero[0], hop(out_zero[1], 1))
    got_one = hop(core_zero[1], 4)
    core_low = core_add(out_low[0], hop(out_low[1], 1))
    share = share + hop(give, 2).astype(jnp.float32)
    out_one = out_kernel(activated, unit(1, 0) + unit(1, 1))
    dyp, core_zero, got_one, core_low, out_one, share = together(
        dyp, core_zero, got_one, core_low, out_one, share
    )

    pre_own, pre_pair, pre_other, stat = act_kernel(
        carried_both,
        [(s * chunk + chunk // 2, unit(s, 1)) for s in range(1, layers)],
        partial,
        slope,
        hidden_pre,
    )

    def other_product(s):
        return dot_t(pre_other, up_chunks[s]).astype(jnp.bfloat16)

    def pair_product(s):
        return (
            dot_t(pre_pair, up_chunks[s]) + from_core[s][tokens:].astype(jnp.float32)
        ).astype(jnp.bfloat16)

    def own_product(s):
        return (
            dot_t(pre_own, up_chunks[s])
            + from_core[s][:tokens].astype(jnp.float32)
            + from_pair[s].astype(jnp.float32)
        ).astype(jnp.bfloat16)

    def share_mp(piece):
        if groups == 2:
            return swap_mp(piece)
        whole = lax.psum(piece.astype(jnp.float32), "mp")
        return whole - piece.astype(jnp.float32)

    to_core, from_core, to_pair, from_pair, grad_mine, grad_got = [
        [None] * layers for _ in range(6)
    ]
    to_core[0] = other_product(0)
    share = share + hop(share.astype(jnp.bfloat16), 4).astype(jnp.float32)
    got_low = hop(core_low[1], 4)
    one_got = hop(out_one[1], 1)
    (
        pre_own, pre_pair, pre_other, to_core, stat, share, activated, out_one, one_got,
        got_low, core_low,
    ) = together(
        pre_own, pre_pair, pre_other, to_core, stat, share, activated, out_one, one_got,
        got_low, core_low,
    )

    holds_low = ((mp_rank ^ (me >> 3)) & 1) == 0

    def swap_held(low, high):
        return swap_mp(jnp.where(holds_low, high, low))

    from_core[0] = hop(to_core[0], 1)
    to_pair[0] = pair_product(0)
    to_core[1] = other_product(1)
    from_core, to_pair, to_core, pre_own, pre_pair, pre_other = together(
        from_core, to_pair, to_core, pre_own, pre_pair, pre_other
    )
    high, pair_one, core_high, got_zero, got_high = [None] * 5
    sum_one, sum_zero, sum_high, sent_zero, sent_one = [None] * 5
    other = half = None
    for step in range(layers + 3):
        if step < layers:
            from_pair[step ^ 1] = hop(to_pair[step], 4)
        if 2 <= step < layers + 2:
            s = (step - 2) ^ 1
            grad_got[s] = share_mp(grad_mine[s])
        if 1 <= step <= layers:
            s = (step - 1) ^ 1
            grad_mine[s] = own_product(s)
        if step + 1 < layers:
            from_core[step + 1] = hop(to_core[step + 1], 1)
            to_pair[step + 1] = pair_product(step + 1)
        if step + 2 < layers:
            to_core[step + 2] = other_product(step + 2)
        if step == 0:
            sum_low = pair_add(core_low[0], got_low, swapped=True) if paired else None
            sum_one, pair_one = whole_add(out_one[0], one_got, got_one)
            stat = [stat[:tokens], stat[tokens : 2 * tokens], stat[2 * tokens :]]
        if step == 1:
            if paired:
                sent_one = swap_held(sum_one, sum_low)
            stat_got = hop(stat[2], 1)
            stat = [stat[0] + stat_got[:tokens], stat[1] + stat_got[tokens:]]
        if step == 2:
            high = out_kernel(activated, sum([unit(s, 1) for s in ends], []))
            stat = stat[0] + hop(stat[1], 4)
        if step == 3:
            core_high = core_add(high[0], hop(high[1], 1))
            stat = stat + swap_mp(stat) if groups == 2 else lax.psum(stat, "mp")
            bit = 8
            while bit < size:
                share = share + hop(share.astype(jnp.bfloat16), bit).astype(jnp.float32)
                bit *= 2
        if step == layers:
            got_zero = hop(pair_one, 4)
            other = hop(share, 2)
            half = jnp.concatenate(
                [jnp.where(is_y, other, share), jnp.where(is_y, share, other)], axis=0
            )
        if step == layers + 1:
            got_high = hop(core_high[1], 4)
            sum_zero = pair_add(core_zero[0], got_zero)
            other = hop(half, 1)
        if step == layers + 2:
            if paired:
                sum_high = pair_add(core_high[0], got_high, swapped=True)
                sent_zero = swap_held(sum_zero, sum_high)
            break
        state = (
            to_core, from_core, to_pair, from_pair, grad_mine, grad_got, high, pair_one, sum_low, core_high,
            got_zero, got_high, sum_one, sum_zero, sent_one, stat, share, other, half,
            pre_own, pre_pair, pre_other, activated, core_zero,
        )
        (
            to_core, from_core, to_pair, from_pair, grad_mine, grad_got, high, pair_one, sum_low, core_high,
            got_zero, got_high, sum_one, sum_zero, sent_one, stat, share, other, half,
            pre_own, pre_pair, pre_other, activated, core_zero,
        ) = together(*state)
    adapter_down_grad = jnp.where(is_core, other, half).T
    adapter_up_grad = jnp.where(is_core, half, other)

    input_grad_second = final_kernel(
        at, size, grad_second, lower_full, gain, inverse_rms, stat, grad_mine, grad_got
    )

    if paired:
        lower_first = first_kernel(
            at,
            size,
            upper_slice,
            [sum_zero, sum_one, sum_low, sum_high],
            [sent_one, sent_zero],
        )
    else:
        width = chunk // 2
        pieces = [sum_zero, sum_one]
        for s in ends:
            for own, got in ((core_low, got_low), (core_high, got_high)):
                mine = own[0][:, (s - 2) * width : (s - 1) * width]
                theirs = got[:, ((s ^ 1) - 2) * width : ((s ^ 1) - 1) * width]
                pieces.append((mine + theirs.astype(jnp.float32)).astype(jnp.bfloat16))
        chunks = pieces[:2] + [
            jnp.concatenate(pieces[i : i + 2], axis=1) for i in range(2, len(pieces), 2)
        ]
        out_whole = restore(at, size, chunks)
        frozen_share = lax.psum_scatter(
            out_whole.astype(jnp.float32), "mp", scatter_dimension=1, tiled=True
        )
        lower_first = ((upper_slice.astype(jnp.float32) - frozen_share) / coupling).astype(
            jnp.bfloat16
        )
    return (
        lower_first,
        lower_second,
        input_grad_first,
        input_grad_second,
        adapter_down_grad,
        adapter_up_grad,
    )


def solution(mesh):
    return jax.shard_map(
        on_device,
        mesh=mesh,
        in_specs=(
            P("dp", None),
            P("dp", None),
            P("dp", None),
            P("dp", None),
            P(),
            P("dp", "mp"),
            P("dp", "mp"),
            P(),
            P(),
        ),
        out_specs=(
            P("dp", "mp"),
            P("dp", "mp"),
            P("dp", "mp"),
            P("dp", None),
            P("mp", None),
            P(None, "mp"),
        ),
        check_vma=False,
    )
```
